128 devices in a mesh: owner: 32 (over y, x, core), replica: 4 (over z).
Axes of the slice: x: 4, y: 4, z: 4, core: 2. Of those that a mesh axis runs over, the one named last changes fastest.
Arguments:
- queries: bfloat16 [4096, 1024], P(('owner', 'replica')), may hold values from -6 to 6
- probes: int32 [4096, 8], P(('owner', 'replica')), may hold values from 0 to 127, as said below
- list_slot: int32 [128], replicated, may hold values from 0 to 127, each once
- valid_rows: int32 [128], P('owner'), may hold values from 128 to 1024
- database: bfloat16 [128, 1024, 1024], P('owner', 'replica'), may hold values from -0.1875 to 0.1875
Outputs:
- nearest: float32 [4096, 32], P(('owner', 'replica'))
The draws below stay inside these ranges and needn't reach their ends.
Inputs may be any that keep to these rules, and one draw needn't show every extreme that they name: `probes`: each query names 8 different lists; in every aligned block of 32 query rows no list is named by more than 4 queries. `list_slot`: each position once.
All inputs are finite; a program needn't handle non-finite values.
Results may differ from the reference program's by a relative error of at most 0.0003.
Values may be sent and summed in bfloat16 or wider, within the bound.
No kernel may reach another device: no remote copies, remote signals or barrier semaphores. Data moves between devices by JAX's collectives and lax.ppermute only.
A program may use at most 64 MiB of HBM per device.

```python
import jax
import jax.numpy as jnp
from jax import lax

D = 1024
ROWS = 1024
PROBES = 8
TOPK = 32
CAPL = 4
LISTS = 128
Q_DEV = 32
QUERIES = 4096
N_OWNER = 32
N_REPLICA = 4


def draw_probes(key, part):
    key = jax.random.fold_in(key, 7)
    groups = LISTS // PROBES
    blocks = QUERIES // Q_DEV
    common_key, block_key = jax.random.split(key)
    shuffled = jax.random.permutation(common_key, LISTS).astype(jnp.int32)
    hot_lists = shuffled[:PROBES]
    others = shuffled[PROBES:]

    def one_block(this_key):
        first_key, second_key, third_key = jax.random.split(this_key, 3)
        picked = jax.random.permutation(first_key, (groups - 1) * CAPL)[:Q_DEV - CAPL]
        group_ids = jnp.concatenate([jnp.zeros((CAPL,), jnp.int32), (picked // CAPL + 1).astype(jnp.int32)])
        group_ids = group_ids[jax.random.permutation(second_key, Q_DEV)]
        mixed = others[jax.random.permutation(third_key, LISTS - PROBES)]
        lookup = jnp.concatenate([hot_lists, mixed])
        list_index = group_ids[:, None] * PROBES + jnp.arange(PROBES, dtype=jnp.int32)[None, :]
        return lookup[list_index]
    block_keys = jax.random.split(block_key, blocks)
    return jax.vmap(one_block)(block_keys).reshape(QUERIES, PROBES).astype(jnp.int32)


def with_ends(drawn, own_key, low, largest):
    spot = [jax.random.randint(jax.random.fold_in(own_key, axis), (), 0, length) for axis, length in enumerate(drawn.shape)]
    widest = drawn.shape.index(max(drawn.shape))
    beside = spot[:widest] + [(spot[widest] + 1) % drawn.shape[widest]] + spot[widest + 1:]
    return drawn.at[tuple(spot)].set(low).at[tuple(beside)].set(largest)


def block_levels(stream_key, dims, cuts, smallest, top_value):
    def one(dim, shards_of):
        heights = jax.random.uniform(jax.random.fold_in(jax.random.fold_in(stream_key, 6), dim), (shards_of,), jnp.float32, smallest / len(cuts), top_value / len(cuts))
        return jnp.repeat(jnp.exp(heights), dims[dim] // shards_of).reshape((-1,) + (1,) * (len(dims) - dim - 1))

    level = one(*cuts[0])
    for cut in cuts[1:]:
        level = level * one(*cut)
    return level


def scatter_about(own_key, extent, scale, reach, shards=(), held_as=jnp.bfloat16):
    drawn = scale * jax.random.normal(own_key, extent, jnp.float32)
    if shards:
        drawn = drawn * block_levels(own_key, extent, shards, -0.22, 0.18)
    return jnp.clip(drawn, -reach, reach).astype(held_as)


def setup_inputs(seed: int = 0) -> dict:
    key_list = jax.random.split(jax.random.key(seed), 6)
    queries = scatter_about(key_list[0], (QUERIES, D), 1.0, 6.0, ((0, 128),))
    probes = draw_probes(jax.random.fold_in(key_list[5], 71), 0)
    list_slot = jax.random.permutation(key_list[2], LISTS).astype(jnp.int32)
    valid_rows = with_ends(jax.random.randint(key_list[3], (LISTS,), ROWS // 8, ROWS + 1), jax.random.fold_in(key_list[3], 1), ROWS // 8, ROWS).astype(jnp.int32)
    database = scatter_about(key_list[4], (LISTS, ROWS, D), D ** -0.5, 0.1875, ((0, 32), (1, 4)))
    return {"queries": queries, "probes": probes, "list_slot": list_slot, "valid_rows": valid_rows, "database": database}


def reference(queries, probes, list_slot, valid_rows, database):
    pair_count = QUERIES * PROBES
    most = N_OWNER * N_REPLICA * CAPL
    positions = list_slot[probes].reshape(-1).astype(jnp.int32)
    pair_ids = jnp.arange(pair_count, dtype=jnp.int32)
    ordering = jnp.argsort(positions * pair_count + pair_ids).astype(jnp.int32)
    counts = jnp.zeros((LISTS,), jnp.int32).at[positions].add(1)
    offsets = (jnp.cumsum(counts) - counts).astype(jnp.int32)
    padded = jnp.concatenate([ordering, jnp.zeros((most,), jnp.int32)])
    row_ids = jnp.arange(ROWS, dtype=jnp.int32)
    slot_ids = jnp.arange(most, dtype=jnp.int32)

    def visit(stored, position):
        chosen = lax.dynamic_slice(padded, (offsets[position].astype(jnp.int32),), (most,))
        is_live = slot_ids < counts[position]
        list_rows = lax.dynamic_index_in_dim(database, position, 0, keepdims=False)
        half_norm = 0.5 * jnp.sum(jnp.square(list_rows.astype(jnp.float32)), -1)
        picked = queries[chosen // PROBES]
        scores = jnp.dot(picked, list_rows.T, preferred_element_type=jnp.float32) - half_norm[None, :]
        scores = jnp.where(row_ids[None, :] < valid_rows[position], scores, -1e30)
        best_vals = lax.top_k(scores, TOPK)[0]
        target = jnp.where(is_live, chosen, pair_count)
        return stored.at[target].set(best_vals, mode="drop"), None

    initial = jnp.zeros((pair_count, TOPK), jnp.float32)
    result, _ = lax.scan(visit, initial, jnp.arange(LISTS, dtype=jnp.int32))
    return lax.top_k(result.reshape(QUERIES, PROBES * TOPK), TOPK)[0]
```

```python
import itertools

import jax
import jax.numpy as jnp
import numpy as np
from jax import lax
from jax.experimental import pallas as pl
from jax.experimental.pallas import tpu as pltpu
from jax.sharding import PartitionSpec as P

D = 1024
WIDE = D + 128
TOPK = 32
AXES = ("owner", "replica")
N_DEV = 128
N_CORE = 64
BIG = 1e30
F32 = jnp.float32
BF16 = jnp.bfloat16

PAIRING = {"a": (1, 0, 3, 2), "b": (3, 2, 1, 0)}
DIMS_A = ("za", "ya", "xa")
DIMS_B = ("zb", "yb", "xb")


def moved(device, dim):
    z, core, x, y = device % 4, device // 4 % 2, device // 8 % 4, device // 32
    place = {"x": x, "y": y, "z": z}
    place[dim[0]] = PAIRING[dim[1]][place[dim[0]]]
    return ((place["y"] * 4 + place["x"]) * 2 + core) * 4 + place["z"]


def core_of(device):
    return device // 4 % 2


def far(device, mask, first):
    dims = DIMS_A if (core_of(device) == 0) == first else DIMS_B
    for bit, dim in enumerate(dims):
        if mask >> bit & 1:
            device = moved(device, dim)
    return device


def near_group(device):
    return tuple(sorted(far(device, mask, True) for mask in range(8)))


NEAR_GROUPS = [list(group) for group in sorted({near_group(device) for device in range(N_DEV)})]
CORE_GROUPS = [[device for device in range(N_DEV) if core_of(device) == core] for core in range(2)]
CORE_SWAP = [(device, device ^ 4) for device in range(N_DEV)]
FIRST_HALF = (0, 1, 2, 4)
SECOND_HALF = (3, 6, 5, 7)


def block_places():
    table = np.zeros((N_DEV, N_CORE), np.int32)
    for device in range(N_DEV):
        owners = itertools.chain.from_iterable(near_group(far(device, mask, False)) for mask in FIRST_HALF + SECOND_HALF)
        table[device] = [owner // 8 * 4 + owner % 4 for owner in owners]
    return table


def sort_pairs(count):
    pairs = []
    p = 1
    while p < count:
        k = p
        while k >= 1:
            for j in range(k % p, count - k, 2 * k):
                for i in range(min(k, count - j - k)):
                    if (i + j) // (p * 2) == (i + j + k) // (p * 2):
                        pairs.append((i + j, i + j + k))
            k //= 2
        p *= 2
    return pairs


SORT_PAIRS = sort_pairs(TOPK)
MERGE_PAIRS = [(i, i + d) for d in (16, 8, 4, 2, 1) for i in range(TOPK) if not i & d]


def exchange(values, pairs):
    values = list(values)
    for i, j in pairs:
        values[i], values[j] = jnp.maximum(values[i], values[j]), jnp.minimum(values[i], values[j])
    return values


def merged(first, second):
    return exchange([jnp.maximum(first[i], second[TOPK - 1 - i]) for i in range(TOPK)], MERGE_PAIRS)


def merged_rows(first, second, shift):
    row = lax.broadcasted_iota(jnp.int32, (8, 128), 0)
    odd = (row & shift) != 0
    here = [jnp.where(odd, b, a) for a, b in zip(first, second)]
    there = [pltpu.roll(jnp.where(odd, a, b), 8 - shift, 0) for a, b in zip(first, second)]
    return merged(here, there)


def place_matrix(slot_ref):
    core = lax.rem(lax.axis_index("owner"), 2)
    places = jnp.bitwise_xor(slot_ref[...], 4 * core)
    return (places == lax.broadcasted_iota(jnp.int32, (128, 128), 0)).astype(BF16)


def rank_table(probes_ref, place):
    probes = probes_ref[...]
    lists = lax.broadcasted_iota(jnp.int32, (32, 128), 1)
    named = jnp.zeros((32, 128), F32)
    for j in range(8):
        named = jnp.where(probes[:, j : j + 1] == lists, 1.0, named)
    probed = lax.dot_general(named.astype(BF16), place, (((1,), (1,)), ((), ())), preferred_element_type=F32)
    before = lax.broadcasted_iota(jnp.int32, (32, 32), 1) < lax.broadcasted_iota(jnp.int32, (32, 32), 0)
    rank = jnp.dot(before.astype(BF16), probed.astype(BF16), preferred_element_type=F32)
    return jnp.where(probed > 0.5, rank, -1.0).astype(BF16)


def widen_kernel(queries_ref, probes_ref, slot_ref, out_ref):
    out_ref[:, :D] = queries_ref[...]
    out_ref[:, D:] = rank_table(probes_ref, place_matrix(slot_ref))


def wanted_kernel(probes_ref, flat_ref, slot_ref, pick_ref, group_ref):
    place = place_matrix(slot_ref)
    rank = rank_table(probes_ref, place)
    named = (flat_ref[...] == lax.broadcasted_iota(jnp.int32, (128, 256), 0)).astype(BF16)
    placed = jnp.dot(place, named, preferred_element_type=F32)
    index = lax.broadcasted_iota(jnp.int32, (128, 256), 0)
    where = jnp.sum(placed * index.astype(F32), 0, keepdims=True).astype(jnp.int32)
    ranks = jnp.dot(rank, placed.astype(BF16), preferred_element_type=F32)
    own = lax.broadcasted_iota(jnp.int32, (32, 256), 0) == (lax.broadcasted_iota(jnp.int32, (32, 256), 1) & 31)
    slot = jnp.sum(jnp.where(own, ranks, 0.0), 0, keepdims=True).astype(jnp.int32)
    row = (where >> 2) * 4 + slot
    pick_ref[...] = (index == row).astype(BF16)
    group_ref[...] = jnp.broadcast_to(where & 3, (8, 256))


def norm_kernel(own_ref, sibling_ref, own_valid_ref, sibling_valid_ref, out_ref):
    first_row = lax.axis_index("replica") * 256
    row = first_row + lax.broadcasted_iota(jnp.int32, (256, 128), 0)
    lane = lax.broadcasted_iota(jnp.int32, (256, 128), 1)
    total = jnp.zeros((256, 128), F32)
    for t in range(8):
        ref, valid = (own_ref, own_valid_ref) if t < 4 else (sibling_ref, sibling_valid_ref)
        rows = ref[t % 4].astype(F32)
        norm = 0.5 * jnp.sum(rows * rows, 1, keepdims=True)
        total = jnp.where(lane == t, jnp.where(row < valid[t % 4], norm, BIG), total)
    out_ref[...] = total


def score_lists(group_refs, own_ref, sibling_ref, norm_ref, block_ref, query_buf, list_buf, chosen, best, sems):
    copies = []
    for g, ref in enumerate(group_refs):
        copies.append(pltpu.make_async_copy(ref, query_buf.at[g], sems.at[g]))
    for t in range(8):
        source = own_ref.at[t] if t < 4 else sibling_ref.at[t - 4]
        copies.append(pltpu.make_async_copy(source, list_buf.at[t], sems.at[4 + t]))
    for copy in copies:
        copy.start()
    chip = lax.axis_index("owner") // 2
    column = lax.broadcasted_iota(jnp.int32, (256, 128), 0)
    wanted = (lax.broadcasted_iota(jnp.int32, (256, 128), 1) == chip * 8 + (column >> 5)).astype(BF16)
    column = lax.broadcasted_iota(jnp.int32, (256, 256), 0)
    same_block = (lax.broadcasted_iota(jnp.int32, (256, 256), 1) >> 5) == (column & 7)
    column_rank = ((column >> 3) & 3).astype(F32)
    for g in range(4):
        copies[g].wait()
        rank = lax.dot_general(wanted, query_buf[g, :, D:], (((1,), (1,)), ((), ())), preferred_element_type=F32)
        pick = (same_block & (rank == column_rank)).astype(BF16)
        picked = jnp.dot(pick, query_buf[g, :, :D], preferred_element_type=F32).astype(BF16)
        for t in range(8):
            chosen[t, 32 * g : 32 * g + 32, :] = picked[32 * t : 32 * t + 32]

    def sorted_list(t):
        copies[4 + t].wait()
        scores = lax.dot_general(list_buf[t], chosen[t], (((1,), (1,)), ((), ())), preferred_element_type=F32)
        scores = scores - norm_ref[:, t : t + 1]
        return exchange([scores[8 * i : 8 * i + 8] for i in range(TOPK)], SORT_PAIRS)

    quads = []
    for quad in range(2):
        pairs = [merged_rows(sorted_list(4 * quad + 2 * p), sorted_list(4 * quad + 2 * p + 1), 1) for p in range(2)]
        quads.append(merged_rows(pairs[0], pairs[1], 2))
    for i, value in enumerate(merged_rows(quads[0], quads[1], 4)):
        best[8 * i : 8 * i + 8, :] = value
    for half in range(2):
        rows = jnp.concatenate([best[pl.ds(4 * half + t, TOPK, stride=8), :] for t in range(4)], 0)
        turned = rows.T
        for g in range(4):
            for k in range(4):
                block_ref[pl.ds(64 * g + 4 * half + k, 8, stride=8), :] = turned[32 * g + 8 * k : 32 * g + 8 * k + 8]


def first_kernel(*refs):
    groups, (own, sibling, norm, out), scratch = refs[:4], refs[4:8], refs[8:]
    score_lists(groups, own, sibling, norm, out, *scratch)


def second_kernel(*refs):
    groups, (own, sibling, norm, earlier, place_ref, out, block_buf), scratch = refs[:4], refs[4:11], refs[11:]
    score_lists(groups, own, sibling, norm, block_buf, *scratch)
    for b in range(32):
        out[place_ref[b]] = earlier[8 * b : 8 * b + 8, :]
        out[place_ref[32 + b]] = block_buf[8 * b : 8 * b + 8, :]


def final_kernel(back_ref, pick_ref, group_ref, out_ref, tiles, rows):
    pick = pick_ref[...]
    group = jnp.concatenate([group_ref[...]] * 4, 0)
    for z in range(4):
        left = back_ref[:, z].reshape(128, 128).T
        found = jnp.zeros((128, 256), F32)
        for _ in range(3):
            piece = left.astype(BF16)
            left = left - piece.astype(F32)
            found = found + jnp.dot(piece, pick, preferred_element_type=F32)
        scores = found[:32]
        for t in range(1, 4):
            scores = jnp.where(group == t, found[32 * t : 32 * t + 32], scores)
        for half in range(2):
            tiles[pl.ds(2 * z + half, TOPK, stride=8), :] = scores[:, 128 * half : 128 * half + 128]
    values = [tiles[8 * i : 8 * i + 8, :] for i in range(TOPK)]
    for axis, shift in ((0, 4), (0, 2), (0, 1), (1, 64), (1, 32)):
        values = merged(values, [pltpu.roll(value, shift, axis) for value in values])
    for i, value in enumerate(values):
        rows[i : i + 1, :] = value[:1]
    out_ref[...] = rows[...].T[:32]


def params():
    return pltpu.CompilerParams(vmem_limit_bytes=40 * 1024 * 1024)


def spaces(text):
    kinds = {"v": pltpu.VMEM, "s": pltpu.SMEM, "a": pl.ANY}
    return [pl.BlockSpec(memory_space=kinds[kind]) for kind in text]


def hop(value, mask):
    return lax.ppermute(value, AXES, [(device, far(device, mask, False)) for device in range(N_DEV)])


def per_device(queries, probes, list_slot, valid_rows, database):
    shape = jax.ShapeDtypeStruct
    slots = list_slot.reshape(1, 128)
    sibling = lax.ppermute(database, AXES, CORE_SWAP)
    sibling_valid = lax.ppermute(valid_rows, AXES, CORE_SWAP)
    wide = pl.pallas_call(
        widen_kernel, out_shape=shape((32, WIDE), BF16), in_specs=spaces("vvv"), out_specs=spaces("v")[0], name="widen"
    )(queries, probes, slots)
    copies = jnp.broadcast_to(wide[None], (8, 32, WIDE))
    near = lax.all_to_all(copies, AXES, 0, 0, axis_index_groups=NEAR_GROUPS, tiled=True).reshape(256, WIDE)
    gathered = {0: near}
    for mask in (1, 2, 4):
        gathered[mask] = hop(near, mask)
    for mask, source, step in ((3, 1, 2), (6, 2, 4), (5, 4, 1)):
        gathered[mask] = hop(gathered[source], step)
    gathered[7] = hop(gathered[3], 4)

    norms = pl.pallas_call(
        norm_kernel, out_shape=shape((256, 128), F32), in_specs=spaces("vvss"), out_specs=spaces("v")[0], name="norms",
        compiler_params=params(),
    )(database, sibling, valid_rows, sibling_valid)
    pick, group = pl.pallas_call(
        wanted_kernel, out_shape=(shape((128, 256), BF16), shape((8, 256), jnp.int32)), in_specs=spaces("vvv"),
        out_specs=spaces("vv"), name="wanted",
    )(probes, probes.T.reshape(1, 256), slots)
    places = jnp.asarray(block_places())[lax.axis_index(AXES)]

    scratch = [
        pltpu.VMEM((4, 256, WIDE), BF16),
        pltpu.VMEM((8, 256, D), BF16),
        pltpu.VMEM((8, 128, D), BF16),
        pltpu.VMEM((256, 128), F32),
        pltpu.SemaphoreType.DMA((12,)),
    ]
    early = pl.pallas_call(
        first_kernel, out_shape=shape((256, 128), F32), in_specs=spaces("aaaaaav"), out_specs=spaces("v")[0],
        scratch_shapes=scratch, compiler_params=params(), name="score_first",
    )(*[gathered[mask] for mask in FIRST_HALF], database, sibling, norms)
    blocks = pl.pallas_call(
        second_kernel, out_shape=shape((N_CORE, 8, 128), F32), in_specs=spaces("aaaaaavvs"), out_specs=spaces("v")[0],
        scratch_shapes=[pltpu.VMEM((256, 128), F32)] + scratch, compiler_params=params(), name="score_second",
    )(*[gathered[mask] for mask in SECOND_HALF], database, sibling, norms, early, places)
    back = lax.all_to_all(blocks, AXES, 0, 0, axis_index_groups=CORE_GROUPS, tiled=True)
    return pl.pallas_call(
        final_kernel, out_shape=shape((32, TOPK), F32), in_specs=spaces("vvv"), out_specs=spaces("v")[0],
        scratch_shapes=[pltpu.VMEM((256, 128), F32), pltpu.VMEM((32, 128), F32)], compiler_params=params(), name="final",
    )(back.reshape(16, 4, 8, 128), pick, group)


def solution(mesh):
    in_specs = (P(AXES, None), P(AXES, None), P(), P("owner"), P("owner", "replica", None))
    return jax.shard_map(per_device, mesh=mesh, in_specs=in_specs, out_specs=P(AXES, None), check_vma=False)
```

```python
import itertools

import jax
import jax.numpy as jnp
import numpy as np
from jax import lax
from jax.experimental import pallas as pl
from jax.experimental.pallas import tpu as pltpu
from jax.sharding import PartitionSpec as P

D = 1024
WIDE = D + 128
TOPK = 32
AXES = ("owner", "replica")
N_DEV = 128
N_CORE = 64
BIG = 1e30
F32 = jnp.float32
BF16 = jnp.bfloat16

PAIRING = {"a": (1, 0, 3, 2), "b": (3, 2, 1, 0)}
DIMS_A = ("za", "ya", "xa")
DIMS_B = ("zb", "yb", "xb")


def moved(device, dim):
    z, core, x, y = device % 4, device // 4 % 2, device // 8 % 4, device // 32
    place = {"x": x, "y": y, "z": z}
    place[dim[0]] = PAIRING[dim[1]][place[dim[0]]]
    return ((place["y"] * 4 + place["x"]) * 2 + core) * 4 + place["z"]


def core_of(device):
    return device // 4 % 2


def far(device, mask, first):
    dims = DIMS_A if (core_of(device) == 0) == first else DIMS_B
    for bit, dim in enumerate(dims):
        if mask >> bit & 1:
            device = moved(device, dim)
    return device


def near_group(device):
    return tuple(sorted(far(device, mask, True) for mask in range(8)))


NEAR_GROUPS = [list(group) for group in sorted({near_group(device) for device in range(N_DEV)})]
CORE_GROUPS = [[device for device in range(N_DEV) if core_of(device) == core] for core in range(2)]
CORE_SWAP = [(device, device ^ 4) for device in range(N_DEV)]
FIRST_HALF = (0, 1, 2, 4)
SECOND_HALF = (3, 6, 5, 7)


THIRDS = ((0, 96), (96, 176), (176, 256))


def block_places():
    table = np.zeros((N_DEV, N_CORE), np.int32)
    for device in range(N_DEV):
        owners = itertools.chain.from_iterable(near_group(far(device, mask, False)) for mask in FIRST_HALF + SECOND_HALF)
        table[device] = [owner // 8 * 4 + owner % 4 for owner in owners]
    return table


def sort_pairs(count):
    pairs = []
    p = 1
    while p < count:
        k = p
        while k >= 1:
            for j in range(k % p, count - k, 2 * k):
                for i in range(min(k, count - j - k)):
                    if (i + j) // (p * 2) == (i + j + k) // (p * 2):
                        pairs.append((i + j, i + j + k))
            k //= 2
        p *= 2
    return pairs


SORT_PAIRS = sort_pairs(TOPK)
MERGE_PAIRS = [(i, i + d) for d in (16, 8, 4, 2, 1) for i in range(TOPK) if not i & d]


def exchange(values, pairs):
    values = list(values)
    for i, j in pairs:
        values[i], values[j] = jnp.maximum(values[i], values[j]), jnp.minimum(values[i], values[j])
    return values


def merged(first, second):
    return exchange([jnp.maximum(first[i], second[TOPK - 1 - i]) for i in range(TOPK)], MERGE_PAIRS)


def merged_rows(first, second, shift):
    row = lax.broadcasted_iota(jnp.int32, (8, 128), 0)
    odd = (row & shift) != 0
    here = [jnp.where(odd, b, a) for a, b in zip(first, second)]
    there = [pltpu.roll(jnp.where(odd, a, b), 8 - shift, 0) for a, b in zip(first, second)]
    return merged(here, there)


def place_matrix(slot_ref):
    core = lax.rem(lax.axis_index("owner"), 2)
    places = jnp.bitwise_xor(slot_ref[...], 4 * core)
    return (places == lax.broadcasted_iota(jnp.int32, (128, 128), 0)).astype(BF16)


def rank_table(probes_ref, place):
    lists = lax.broadcasted_iota(jnp.int32, (128, 32), 0)
    named = jnp.zeros((128, 32), F32)
    for j in range(8):
        named = jnp.where(probes_ref[j : j + 1, :] == lists, 1.0, named)
    probed = jnp.dot(place, named.astype(BF16), preferred_element_type=F32)
    before = lax.broadcasted_iota(jnp.int32, (32, 32), 0) < lax.broadcasted_iota(jnp.int32, (32, 32), 1)
    rank = jnp.dot(probed.astype(BF16), before.astype(BF16), preferred_element_type=F32)
    return jnp.where(probed > 0.5, rank, -1.0)


def widen_kernel(queries_ref, probes_ref, slot_ref, out_ref):
    table = rank_table(probes_ref, place_matrix(slot_ref)).T.astype(BF16)
    for copy in range(8):
        out_ref[copy, :, :D] = queries_ref[...]
        out_ref[copy, :, D:] = table


def wanted_kernel(probes_ref, slot_ref, pick_ref, group_ref):
    place = place_matrix(slot_ref)
    rank = rank_table(probes_ref, place)
    index = lax.broadcasted_iota(jnp.int32, (128, 32), 0)
    for j in range(8):
        placed = jnp.dot(place, (probes_ref[j : j + 1, :] == index).astype(BF16), preferred_element_type=F32)
        where = jnp.sum(placed * index.astype(F32), 0, keepdims=True).astype(jnp.int32)
        slot = jnp.sum(placed * rank, 0, keepdims=True).astype(jnp.int32)
        pick_ref[:, 32 * j : 32 * j + 32] = (index == (where >> 2) * 4 + slot).astype(BF16)
        group_ref[:, 32 * j : 32 * j + 32] = jnp.broadcast_to(where & 3, (8, 32))


def norm_kernel(own_ref, sibling_ref, own_valid_ref, sibling_valid_ref, out_ref):
    first_row = lax.axis_index("replica") * 256
    row = first_row + lax.broadcasted_iota(jnp.int32, (256, 128), 0)
    lane = lax.broadcasted_iota(jnp.int32, (256, 128), 1)
    total = jnp.zeros((256, 128), F32)
    for t in range(8):
        ref, valid = (own_ref, own_valid_ref) if t < 4 else (sibling_ref, sibling_valid_ref)
        rows = ref[t % 4].astype(F32)
        norm = 0.5 * jnp.sum(rows * rows, 1, keepdims=True)
        total = jnp.where(lane == t, jnp.where(row < valid[t % 4], norm, BIG), total)
    out_ref[...] = total


def score_lists(group_refs, own_ref, sibling_ref, norm_ref, block_ref, chosen, best):
    chip = lax.axis_index("owner") // 2
    column = lax.broadcasted_iota(jnp.int32, (256, 128), 0)
    wanted = (lax.broadcasted_iota(jnp.int32, (256, 128), 1) == chip * 8 + (column >> 5)).astype(BF16)
    column = lax.broadcasted_iota(jnp.int32, (256, 256), 0)
    same_block = (lax.broadcasted_iota(jnp.int32, (256, 256), 1) >> 5) == (column & 7)
    column_rank = ((column >> 3) & 3).astype(F32)
    for g in range(4):
        ref = group_refs[g]
        rank = lax.dot_general(wanted, ref[:, D:], (((1,), (1,)), ((), ())), preferred_element_type=F32)
        pick = (same_block & (rank == column_rank)).astype(BF16)
        picked = jnp.dot(pick, ref[:, :D], preferred_element_type=F32).astype(BF16)
        for t in range(8):
            chosen[t, 32 * g : 32 * g + 32, :] = picked[32 * t : 32 * t + 32]

    def sorted_list(t):
        rows = own_ref[t] if t < 4 else sibling_ref[t - 4]
        scores = lax.dot_general(rows, chosen[t], (((1,), (1,)), ((), ())), preferred_element_type=F32)
        scores = scores - norm_ref[:, t : t + 1]
        return exchange([scores[8 * i : 8 * i + 8] for i in range(TOPK)], SORT_PAIRS)

    quads = []
    for quad in range(2):
        pairs = [merged_rows(sorted_list(4 * quad + 2 * p), sorted_list(4 * quad + 2 * p + 1), 1) for p in range(2)]
        quads.append(merged_rows(pairs[0], pairs[1], 2))
    for i, value in enumerate(merged_rows(quads[0], quads[1], 4)):
        best[8 * i : 8 * i + 8, :] = value
    for half in range(2):
        rows = jnp.concatenate([best[pl.ds(4 * half + t, TOPK, stride=8), :] for t in range(4)], 0)
        turned = rows.T
        for g in range(4):
            for k in range(4):
                block_ref[pl.ds(64 * g + 4 * half + k, 8, stride=8), :] = turned[32 * g + 8 * k : 32 * g + 8 * k + 8]


def first_kernel(*refs):
    groups, (own, sibling, norm, out), scratch = refs[:4], refs[4:8], refs[8:]
    score_lists(groups, own, sibling, norm, out, *scratch)


def second_kernel(*refs):
    groups, pieces, (own, sibling, norm, earlier, place_ref, out, last, block_buf), scratch = refs[:3], refs[3:6], refs[6:14], refs[14:]
    for piece, (start, stop) in zip(pieces, THIRDS):
        last[start:stop, :] = piece[...]
    score_lists(groups + (last,), own, sibling, norm, block_buf, *scratch)
    for b in range(32):
        out[place_ref[b]] = earlier[8 * b : 8 * b + 8, :]
        out[place_ref[32 + b]] = block_buf[8 * b : 8 * b + 8, :]


def final_kernel(back_ref, pick_ref, group_ref, out_ref, tiles, rows):
    pick = pick_ref[...]
    group = jnp.concatenate([group_ref[...]] * 4, 0)
    for z in range(4):
        left = back_ref[:, z].reshape(128, 128).T
        found = jnp.zeros((128, 256), F32)
        for _ in range(3):
            piece = left.astype(BF16)
            left = left - piece.astype(F32)
            found = found + jnp.dot(piece, pick, preferred_element_type=F32)
        scores = found[:32]
        for t in range(1, 4):
            scores = jnp.where(group == t, found[32 * t : 32 * t + 32], scores)
        for half in range(2):
            tiles[pl.ds(2 * z + half, TOPK, stride=8), :] = scores[:, 128 * half : 128 * half + 128]
    values = [tiles[8 * i : 8 * i + 8, :] for i in range(TOPK)]
    for axis, shift in ((0, 4), (0, 2), (0, 1), (1, 64), (1, 32)):
        values = merged(values, [pltpu.roll(value, shift, axis) for value in values])
    for i, value in enumerate(values):
        rows[i : i + 1, :] = value[:1]
    out_ref[...] = rows[...].T[:32]


def params():
    return pltpu.CompilerParams(vmem_limit_bytes=20 * 1024 * 1024)


def spaces(text):
    kinds = {"v": pltpu.VMEM, "s": pltpu.SMEM, "a": pl.ANY}
    return [pl.BlockSpec(memory_space=kinds[kind]) for kind in text]


def hop(value, mask):
    return lax.ppermute(value, AXES, [(device, far(device, mask, False)) for device in range(N_DEV)])


def per_device(queries, probes, list_slot, valid_rows, database):
    shape = jax.ShapeDtypeStruct
    slots = list_slot.reshape(1, 128)
    probes = probes.T
    wide = pl.pallas_call(
        widen_kernel, out_shape=shape((8, 32, WIDE), BF16), in_specs=spaces("vvv"), out_specs=spaces("v")[0], name="widen"
    )(queries, probes, slots)
    near = lax.all_to_all(wide, AXES, 0, 0, axis_index_groups=NEAR_GROUPS, tiled=True).reshape(256, WIDE)
    sibling = lax.ppermute(database, AXES, CORE_SWAP)
    sibling_valid = lax.ppermute(valid_rows, AXES, CORE_SWAP)
    pick, group = pl.pallas_call(
        wanted_kernel, out_shape=(shape((128, 256), BF16), shape((8, 256), jnp.int32)), in_specs=spaces("vv"),
        out_specs=spaces("vv"), name="wanted",
    )(probes, slots)
    places = jnp.asarray(block_places())[lax.axis_index(AXES)]
    near, pick, group, places = lax.optimization_barrier((near, pick, group, places))

    gathered = {0: near}
    for mask in (1, 2, 4):
        gathered[mask] = hop(near, mask)
    norms = pl.pallas_call(
        norm_kernel, out_shape=shape((256, 128), F32), in_specs=spaces("vvss"), out_specs=spaces("v")[0], name="norms",
        compiler_params=params(),
    )(database, sibling, valid_rows, sibling_valid)
    gathered[1], gathered[2], gathered[4], norms = lax.optimization_barrier((gathered[1], gathered[2], gathered[4], norms))

    for mask, source, step in ((3, 1, 2), (6, 2, 4), (5, 4, 1)):
        gathered[mask] = hop(gathered[source], step)
    scratch = [pltpu.VMEM((8, 128, D), BF16), pltpu.VMEM((256, 128), F32)]
    early = pl.pallas_call(
        first_kernel, out_shape=shape((256, 128), F32), in_specs=spaces("vvvvvvv"), out_specs=spaces("v")[0],
        scratch_shapes=scratch, compiler_params=params(), name="score_first",
    )(*[gathered[mask] for mask in FIRST_HALF], database, sibling, norms)
    gathered[3], gathered[6], gathered[5], early = lax.optimization_barrier((gathered[3], gathered[6], gathered[5], early))

    last = [hop(gathered[source][start:stop], step) for (source, step), (start, stop) in zip(((3, 4), (6, 1), (5, 2)), THIRDS)]
    blocks = pl.pallas_call(
        second_kernel, out_shape=shape((N_CORE, 8, 128), F32), in_specs=spaces("vvvvvvvvvvs"), out_specs=spaces("v")[0],
        scratch_shapes=[pltpu.VMEM((256, WIDE), BF16), pltpu.VMEM((256, 128), F32)] + scratch,
        compiler_params=params(), name="score_second",
    )(*[gathered[mask] for mask in SECOND_HALF[:3]], *last, database, sibling, norms, early, places)
    back = lax.all_to_all(blocks, AXES, 0, 0, axis_index_groups=CORE_GROUPS, tiled=True)
    return pl.pallas_call(
        final_kernel, out_shape=shape((32, TOPK), F32), in_specs=spaces("vvv"), out_specs=spaces("v")[0],
        scratch_shapes=[pltpu.VMEM((256, 128), F32), pltpu.VMEM((32, 128), F32)], compiler_params=params(), name="final",
    )(back.reshape(16, 4, 8, 128), pick, group)


def solution(mesh):
    in_specs = (P(AXES, None), P(AXES, None), P(), P("owner"), P("owner", "replica", None))
    return jax.shard_map(per_device, mesh=mesh, in_specs=in_specs, out_specs=P(AXES, None), check_vma=False)
```

```python
import jax
import jax.numpy as jnp
from jax import lax
from jax.experimental import pallas as pl
from jax.experimental.pallas import tpu as pltpu
from jax.sharding import PartitionSpec as P

D = 1024
WIDE = D + 128
TOPK = 32
AXES = ("owner", "replica")
N_DEV = 128
N_CORE = 64
BIG = 1e30
F32 = jnp.float32
BF16 = jnp.bfloat16

PAIRING = {"a": (1, 0, 3, 2), "b": (3, 2, 1, 0)}
DIMS_A = ("za", "ya", "xa")
DIMS_B = ("zb", "yb", "xb")


def moved(device, dim):
    z, core, x, y = device % 4, device // 4 % 2, device // 8 % 4, device // 32
    place = {"x": x, "y": y, "z": z}
    place[dim[0]] = PAIRING[dim[1]][place[dim[0]]]
    return ((place["y"] * 4 + place["x"]) * 2 + core) * 4 + place["z"]


def core_of(device):
    return device // 4 % 2


def dims_of(core, first):
    return DIMS_A if (core == 0) == first else DIMS_B


def far(device, mask, first):
    for bit, dim in enumerate(dims_of(core_of(device), first)):
        if mask >> bit & 1:
            device = moved(device, dim)
    return device


def at_address(core, address):
    return far(far(4 * core, address >> 3, False), address & 7, True)


CORE_GROUPS = [[at_address(core, address) for address in range(N_CORE)] for core in range(2)]
NEAR_GROUPS = [group[start : start + 8] for group in CORE_GROUPS for start in range(0, N_CORE, 8)]
CORE_SWAP = [(device, device ^ 4) for device in range(N_DEV)]
FIRST_HALF = (0, 1, 2, 4)
SECOND_HALF = (3, 6, 5)


def pairing_bits(place, core):
    low, high = (place ^ (place >> 1)) & 1, place >> 1
    even = jnp.equal(core, 0)
    return jnp.where(even, low, high), jnp.where(even, high, low)


def own_group():
    owner = lax.axis_index("owner")
    bits = [pairing_bits(place, owner & 1)[1] for place in (lax.axis_index("replica"), owner >> 3, (owner >> 1) & 3)]
    return bits[0] + 2 * bits[1] + 4 * bits[2]


def sort_pairs(count):
    pairs = []
    p = 1
    while p < count:
        k = p
        while k >= 1:
            for j in range(k % p, count - k, 2 * k):
                for i in range(min(k, count - j - k)):
                    if (i + j) // (p * 2) == (i + j + k) // (p * 2):
                        pairs.append((i + j, i + j + k))
            k //= 2
        p *= 2
    return pairs


SORT_PAIRS = sort_pairs(TOPK)
MERGE_PAIRS = [(i, i + d) for d in (16, 8, 4, 2, 1) for i in range(TOPK) if not i & d]


def exchange(values, pairs):
    values = list(values)
    for i, j in pairs:
        values[i], values[j] = jnp.maximum(values[i], values[j]), jnp.minimum(values[i], values[j])
    return values


def merged(first, second):
    return exchange([jnp.maximum(first[i], second[TOPK - 1 - i]) for i in range(TOPK)], MERGE_PAIRS)


def merged_rows(first, second, shift):
    row = lax.broadcasted_iota(jnp.int32, (8, 128), 0)
    odd = (row & shift) != 0
    here = [jnp.where(odd, b, a) for a, b in zip(first, second)]
    there = [pltpu.roll(jnp.where(odd, a, b), 8 - shift, 0) for a, b in zip(first, second)]
    return merged(here, there)


def place_matrix(slot_ref):
    core = lax.rem(lax.axis_index("owner"), 2)
    places = jnp.bitwise_xor(slot_ref[...], 4 * core)
    return (places == lax.broadcasted_iota(jnp.int32, (128, 128), 0)).astype(BF16)


def rank_table(probes_ref, place):
    lists = lax.broadcasted_iota(jnp.int32, (128, 32), 0)
    named = jnp.zeros((128, 32), F32)
    for j in range(8):
        named = jnp.where(probes_ref[j : j + 1, :] == lists, 1.0, named)
    probed = jnp.dot(place, named.astype(BF16), preferred_element_type=F32)
    before = lax.broadcasted_iota(jnp.int32, (32, 32), 0) < lax.broadcasted_iota(jnp.int32, (32, 32), 1)
    rank = jnp.dot(probed.astype(BF16), before.astype(BF16), preferred_element_type=F32)
    return jnp.where(probed > 0.5, rank, -1.0)


def widen_kernel(queries_ref, probes_ref, slot_ref, out_ref):
    table = rank_table(probes_ref, place_matrix(slot_ref)).T.astype(BF16)
    for copy in range(8):
        out_ref[copy, :, :D] = queries_ref[...]
        out_ref[copy, :, D:] = table


def wanted_kernel(probes_ref, slot_ref, pick_ref, group_ref):
    place = place_matrix(slot_ref)
    rank = rank_table(probes_ref, place)
    index = lax.broadcasted_iota(jnp.int32, (128, 32), 0)
    core = lax.axis_index("owner") & 1
    for j in range(8):
        placed = jnp.dot(place, (probes_ref[j : j + 1, :] == index).astype(BF16), preferred_element_type=F32)
        where = jnp.sum(placed * index.astype(F32), 0, keepdims=True).astype(jnp.int32)
        slot = jnp.sum(placed * rank, 0, keepdims=True).astype(jnp.int32)
        chip = where >> 3
        (y_first, y_second), (x_first, x_second) = [pairing_bits(place, core) for place in (chip >> 2, chip & 3)]
        row = (x_second * 8 + y_second * 4 + x_first * 2 + y_first) * 8 + (where & 4) + slot
        pick_ref[:, 32 * j : 32 * j + 32] = (index == row).astype(BF16)
        group_ref[:, 32 * j : 32 * j + 32] = jnp.broadcast_to(where & 3, (8, 32))


def lists_kernel(own, sibling, own_valid, sibling_valid, lists, norms, sems):
    copies = []
    for t in range(8):
        copies.append(pltpu.make_async_copy(own.at[t] if t < 4 else sibling.at[t - 4], lists.at[t], sems.at[t]))
        copies[t].start()
    row = lax.axis_index("replica") * 256 + lax.broadcasted_iota(jnp.int32, (256, 1), 0)
    lane = lax.broadcasted_iota(jnp.int32, (256, 128), 1)
    total = jnp.zeros((256, 128), F32)
    for t in (4, 5, 6, 7, 0, 1, 2, 3):
        copies[t].wait()
        rows = lists[t].astype(F32)
        valid = (own_valid if t < 4 else sibling_valid)[0:1, t % 4 : t % 4 + 1]
        norm = jnp.where(row < valid, 0.5 * jnp.sum(rows * rows, 1, keepdims=True), BIG)
        total = jnp.where(lane == t, norm, total)
    norms[...] = total


def chosen_queries(wide):
    chip = lax.axis_index("owner") // 2
    column = lax.broadcasted_iota(jnp.int32, (256, 128), 0)
    wanted = (lax.broadcasted_iota(jnp.int32, (256, 128), 1) == chip * 8 + (column >> 5)).astype(BF16)
    rank = lax.dot_general(wanted, wide[:, D:], (((1,), (1,)), ((), ())), preferred_element_type=F32)
    column = lax.broadcasted_iota(jnp.int32, (256, 256), 0)
    same_block = (lax.broadcasted_iota(jnp.int32, (256, 256), 1) >> 5) == ((column >> 2) & 7)
    pick = (same_block & (rank == (column & 3).astype(F32))).astype(BF16)
    return jnp.dot(pick, wide[:, :D], preferred_element_type=F32).astype(BF16)


def score(lists, norms, t, queries):
    return lax.dot_general(lists[t], queries, (((1,), (1,)), ((), ())), preferred_element_type=F32) - norms[:, t : t + 1]


def sort_rows(scores):
    return exchange([scores[8 * i : 8 * i + 8] for i in range(TOPK)], SORT_PAIRS)


def score_kernel(*refs):
    groups, (lists, norms, out, chosen, best) = refs[:-5], refs[-5:]
    if len(groups) < 4:
        chosen[:, 32 * len(groups) :, :] = jnp.zeros((8, 128 - 32 * len(groups), D), BF16)
    for g, ref in enumerate(groups):
        picked = chosen_queries(ref[...])
        for t in range(8):
            chosen[t, 32 * g : 32 * g + 32, :] = picked[32 * t : 32 * t + 32]
    quads = []
    for quad in range(2):
        sets = [sort_rows(score(lists, norms, t, chosen[t])) for t in range(4 * quad, 4 * quad + 4)]
        quads.append(merged_rows(merged_rows(sets[0], sets[1], 1), merged_rows(sets[2], sets[3], 1), 2))
    for i, value in enumerate(merged_rows(quads[0], quads[1], 4)):
        best[8 * i : 8 * i + 8, :] = value
    for half in range(2):
        out[half] = jnp.concatenate([best[pl.ds(4 * half + t, TOPK, stride=8), :] for t in range(4)], 0).T


def last_kernel(lower, upper, lists, norms, first, second, out, best):
    picked = chosen_queries(jnp.concatenate([lower[...], upper[...]], 0))
    lane = lax.broadcasted_iota(jnp.int32, (256, 128), 1)
    sets = []
    for half in range(2):
        queries = picked[128 * half : 128 * half + 128]
        scores = score(lists, norms, 4 * half, queries)
        for t in range(1, 4):
            scores = jnp.where((lane >> 5) == t, score(lists, norms, 4 * half + t, queries), scores)
        sets.append(sort_rows(scores))
    values = merged_rows(sets[0], sets[1], 1)
    for shift in (2, 4):
        values = merged(values, [pltpu.roll(value, 8 - shift, 0) for value in values])
    for i, value in enumerate(values):
        best[8 * i : 8 * i + 8, :] = value
    own = own_group()
    for half in range(2):
        rows = best[pl.ds(half, TOPK, stride=8), :]
        turned = jnp.concatenate([rows] + [pltpu.roll(rows, 128 - 32 * t, 1) for t in range(1, 4)], 0).T
        found = [(mask, first[half, 32 * g : 32 * g + 32, :]) for g, mask in enumerate(FIRST_HALF)]
        found += [(mask, second[half, 32 * g : 32 * g + 32, :]) for g, mask in enumerate(SECOND_HALF)]
        for mask, values in found + [(7, turned[:32])]:
            place = (own ^ mask) * 8
            for b in range(8):
                out[place + b, 4 * half : 4 * half + 4, :] = values[4 * b : 4 * b + 4]


def final_kernel(back_ref, pick_ref, group_ref, out_ref, tiles, rows):
    pick = pick_ref[...]
    group = jnp.concatenate([group_ref[...]] * 4, 0)
    for z in range(4):
        left = back_ref[:, z >> 1, :, z & 1].reshape(128, 128).T
        found = jnp.zeros((128, 256), F32)
        for _ in range(3):
            piece = left.astype(BF16)
            left = left - piece.astype(F32)
            found = found + jnp.dot(piece, pick, preferred_element_type=F32)
        scores = found[:32]
        for t in range(1, 4):
            scores = jnp.where(group == t, found[32 * t : 32 * t + 32], scores)
        for half in range(2):
            tiles[pl.ds(2 * z + half, TOPK, stride=8), :] = scores[:, 128 * half : 128 * half + 128]
    values = [tiles[8 * i : 8 * i + 8, :] for i in range(TOPK)]
    for axis, shift in ((0, 4), (0, 2), (0, 1), (1, 64), (1, 32)):
        values = merged(values, [pltpu.roll(value, shift, axis) for value in values])
    for i, value in enumerate(values):
        rows[i : i + 1, :] = value[:1]
    out_ref[...] = rows[...].T[:32]


def params():
    return pltpu.CompilerParams(vmem_limit_bytes=20 * 1024 * 1024)


def spaces(text):
    kinds = {"v": pltpu.VMEM, "s": pltpu.SMEM, "h": pltpu.HBM, "a": pl.ANY}
    return [pl.BlockSpec(memory_space=kinds[kind]) for kind in text]


def hop(value, mask):
    return lax.ppermute(value, AXES, [(device, far(device, mask, False)) for device in range(N_DEV)])


def per_device(queries, probes, list_slot, valid_rows, database):
    shape = jax.ShapeDtypeStruct
    slots = list_slot.reshape(1, 128)
    probes = probes.T
    wide = pl.pallas_call(
        widen_kernel, out_shape=shape((8, 32, WIDE), BF16), in_specs=spaces("vvv"), out_specs=spaces("v")[0], name="widen"
    )(queries, probes, slots)
    near = lax.all_to_all(wide, AXES, 0, 0, axis_index_groups=NEAR_GROUPS, tiled=True).reshape(256, WIDE)
    sibling = lax.ppermute(database, AXES, CORE_SWAP)
    sibling_valid = lax.ppermute(valid_rows, AXES, CORE_SWAP)
    near, sibling, sibling_valid = lax.optimization_barrier((near, sibling, sibling_valid))

    groups = {0: near}
    for mask in (1, 2, 4):
        groups[mask] = hop(near, mask)
    lists, norms = pl.pallas_call(
        lists_kernel, out_shape=(pltpu.VMEM((8, 256, D), BF16), pltpu.VMEM((256, 128), F32)), in_specs=spaces("havv"),
        out_specs=spaces("vv"), scratch_shapes=[pltpu.SemaphoreType.DMA((8,))], compiler_params=params(), name="lists",
    )(pltpu.with_memory_space_constraint(database, pltpu.HBM), sibling, valid_rows.reshape(1, 4), sibling_valid.reshape(1, 4))
    groups[4], lists, norms = lax.optimization_barrier((groups[4], lists, norms))
    for mask, source, step in ((3, 1, 2), (6, 2, 4), (5, 4, 1)):
        groups[mask] = hop(groups[source], step)

    def scored(masks, name):
        return pl.pallas_call(
            score_kernel, out_shape=shape((2, 128, 128), F32), in_specs=spaces("v" * (len(masks) + 2)), out_specs=spaces("v")[0],
            scratch_shapes=[pltpu.VMEM((8, 128, D), BF16), pltpu.VMEM((256, 128), F32)], compiler_params=params(), name=name,
        )(*[groups[mask] for mask in masks], lists, norms)

    first = scored(FIRST_HALF, "score_first")
    groups[3], groups[6], groups[5], first = lax.optimization_barrier((groups[3], groups[6], groups[5], first))
    last = [hop(groups[3][:128], 4), hop(groups[6][128:], 1)]
    second = scored(SECOND_HALF, "score_second")
    *last, second = lax.optimization_barrier((*last, second))
    blocks = pl.pallas_call(
        last_kernel, out_shape=shape((N_CORE, 8, 128), F32), in_specs=spaces("vvvvvv"), out_specs=spaces("v")[0],
        scratch_shapes=[pltpu.VMEM((256, 128), F32)], compiler_params=params(), name="score_last",
    )(*last, lists, norms, first, second)
    pick, group = pl.pallas_call(
        wanted_kernel, out_shape=(pltpu.VMEM((128, 256), BF16), pltpu.VMEM((8, 256), jnp.int32)), in_specs=spaces("vv"),
        out_specs=spaces("vv"), name="wanted",
    )(probes, slots)
    back = lax.all_to_all(blocks, AXES, 0, 0, axis_index_groups=CORE_GROUPS, tiled=True)
    return pl.pallas_call(
        final_kernel, out_shape=shape((32, TOPK), F32), in_specs=spaces("vvv"), out_specs=spaces("v")[0],
        scratch_shapes=[pltpu.VMEM((256, 128), F32), pltpu.VMEM((32, 128), F32)], compiler_params=params(), name="final",
    )(back.reshape(4, 2, 4, 2, 8, 128), pick, group)


def solution(mesh):
    in_specs = (P(AXES, None), P(AXES, None), P(), P("owner"), P("owner", "replica", None))
    return jax.shard_map(per_device, mesh=mesh, in_specs=in_specs, out_specs=P(AXES, None), check_vma=False)
```

```python
import jax
import jax.numpy as jnp
from jax import lax
from jax.experimental import pallas as pl
from jax.experimental.pallas import tpu as pltpu
from jax.sharding import PartitionSpec as P

D = 1024
WIDE = D + 128
TOPK = 32
AXES = ("owner", "replica")
N_DEV = 128
N_CORE = 64
BIG = 1e30
F32 = jnp.float32
BF16 = jnp.bfloat16

PAIRING = {"a": (1, 0, 3, 2), "b": (3, 2, 1, 0)}
DIMS_A = ("za", "ya", "xb")
DIMS_B = ("zb", "yb", "xa")


def moved(device, dim):
    z, core, x, y = device % 4, device // 4 % 2, device // 8 % 4, device // 32
    place = {"x": x, "y": y, "z": z}
    place[dim[0]] = PAIRING[dim[1]][place[dim[0]]]
    return ((place["y"] * 4 + place["x"]) * 2 + core) * 4 + place["z"]


def core_of(device):
    return device // 4 % 2


def dims_of(core, first):
    return DIMS_A if (core == 0) == first else DIMS_B


def far(device, mask, first):
    for bit, dim in enumerate(dims_of(core_of(device), first)):
        if mask >> bit & 1:
            device = moved(device, dim)
    return device


def at_address(core, address):
    return far(far(4 * core, address >> 3, False), address & 7, True)


CORE_GROUPS = [[at_address(core, address) for address in range(N_CORE)] for core in range(2)]
NEAR_GROUPS = [group[start : start + 8] for group in CORE_GROUPS for start in range(0, N_CORE, 8)]
CORE_SWAP = [(device, device ^ 4) for device in range(N_DEV)]
FIRST_HALF = (0, 1, 2, 4)
SECOND_HALF = (5, 3, 6)


def pairing_bits(place, core, axis):
    low, high = (place ^ (place >> 1)) & 1, place >> 1
    low_first = jnp.equal(core, 0 if axis + "a" in DIMS_A else 1)
    return jnp.where(low_first, low, high), jnp.where(low_first, high, low)


def own_group():
    owner = lax.axis_index("owner")
    places = {"z": lax.axis_index("replica"), "y": owner >> 3, "x": (owner >> 1) & 3}
    z, y, x = [pairing_bits(place, owner & 1, axis)[1] for axis, place in places.items()]
    return z + 2 * y + 4 * x


def sort_pairs(count):
    pairs = []
    p = 1
    while p < count:
        k = p
        while k >= 1:
            for j in range(k % p, count - k, 2 * k):
                for i in range(min(k, count - j - k)):
                    if (i + j) // (p * 2) == (i + j + k) // (p * 2):
                        pairs.append((i + j, i + j + k))
            k //= 2
        p *= 2
    return pairs


SORT_PAIRS = sort_pairs(TOPK)
MERGE_PAIRS = [(i, i + d) for d in (16, 8, 4, 2, 1) for i in range(TOPK) if not i & d]


def exchange(values, pairs):
    values = list(values)
    for i, j in pairs:
        values[i], values[j] = jnp.maximum(values[i], values[j]), jnp.minimum(values[i], values[j])
    return values


def merged(first, second):
    return exchange([jnp.maximum(first[i], second[TOPK - 1 - i]) for i in range(TOPK)], MERGE_PAIRS)


def merged_rows(first, second, shift):
    row = lax.broadcasted_iota(jnp.int32, (8, 128), 0)
    odd = (row & shift) != 0
    here = [jnp.where(odd, b, a) for a, b in zip(first, second)]
    there = [pltpu.roll(jnp.where(odd, a, b), 8 - shift, 0) for a, b in zip(first, second)]
    return merged(here, there)


def place_matrix(slot_ref):
    core = lax.rem(lax.axis_index("owner"), 2)
    places = jnp.bitwise_xor(slot_ref[...], 4 * core)
    return (places == lax.broadcasted_iota(jnp.int32, (128, 128), 0)).astype(BF16)


def rank_table(probes_ref, place):
    lists = lax.broadcasted_iota(jnp.int32, (128, 32), 0)
    named = jnp.zeros((128, 32), F32)
    for j in range(8):
        named = jnp.where(probes_ref[j : j + 1, :] == lists, 1.0, named)
    probed = jnp.dot(place, named.astype(BF16), preferred_element_type=F32)
    before = lax.broadcasted_iota(jnp.int32, (32, 32), 0) < lax.broadcasted_iota(jnp.int32, (32, 32), 1)
    rank = jnp.dot(probed.astype(BF16), before.astype(BF16), preferred_element_type=F32)
    return jnp.where(probed > 0.5, rank, -1.0)


def widen_kernel(queries_ref, probes_ref, slot_ref, out_ref):
    table = rank_table(probes_ref, place_matrix(slot_ref)).T.astype(BF16)
    for copy in range(8):
        out_ref[copy, :, :D] = queries_ref[...]
        out_ref[copy, :, D:] = table


def wanted_kernel(probes_ref, slot_ref, pick_ref, group_ref):
    place = place_matrix(slot_ref)
    rank = rank_table(probes_ref, place)
    index = lax.broadcasted_iota(jnp.int32, (128, 32), 0)
    core = lax.axis_index("owner") & 1
    for j in range(8):
        placed = jnp.dot(place, (probes_ref[j : j + 1, :] == index).astype(BF16), preferred_element_type=F32)
        where = jnp.sum(placed * index.astype(F32), 0, keepdims=True).astype(jnp.int32)
        slot = jnp.sum(placed * rank, 0, keepdims=True).astype(jnp.int32)
        chip = where >> 3
        y_first, y_second = pairing_bits(chip >> 2, core, "y")
        x_first, x_second = pairing_bits(chip & 3, core, "x")
        row = (x_second * 8 + y_second * 4 + x_first * 2 + y_first) * 8 + (where & 4) + slot
        pick_ref[:, 32 * j : 32 * j + 32] = (index == row).astype(BF16)
        group_ref[:, 32 * j : 32 * j + 32] = jnp.broadcast_to(where & 3, (8, 32))


def lists_kernel(own, sibling, own_valid, sibling_valid, lists, norms, sems):
    copies = []
    for t in range(8):
        copies.append(pltpu.make_async_copy(own.at[t] if t < 4 else sibling.at[t - 4], lists.at[t], sems.at[t]))
        copies[t].start()
    row = lax.axis_index("replica") * 256 + lax.broadcasted_iota(jnp.int32, (256, 1), 0)
    lane = lax.broadcasted_iota(jnp.int32, (256, 128), 1)
    total = jnp.zeros((256, 128), F32)
    for t in (4, 5, 6, 7, 0, 1, 2, 3):
        copies[t].wait()
        rows = lists[t].astype(F32)
        valid = (own_valid if t < 4 else sibling_valid)[0:1, t % 4 : t % 4 + 1]
        norm = jnp.where(row < valid, 0.5 * jnp.sum(rows * rows, 1, keepdims=True), BIG)
        total = jnp.where(lane == t, norm, total)
    norms[...] = total


def chosen_queries(wide):
    chip = lax.axis_index("owner") // 2
    column = lax.broadcasted_iota(jnp.int32, (256, 128), 0)
    wanted = (lax.broadcasted_iota(jnp.int32, (256, 128), 1) == chip * 8 + (column >> 5)).astype(BF16)
    rank = lax.dot_general(wanted, wide[:, D:], (((1,), (1,)), ((), ())), preferred_element_type=F32)
    column = lax.broadcasted_iota(jnp.int32, (256, 256), 0)
    same_block = (lax.broadcasted_iota(jnp.int32, (256, 256), 1) >> 5) == ((column >> 2) & 7)
    pick = (same_block & (rank == (column & 3).astype(F32))).astype(BF16)
    return jnp.dot(pick, wide[:, :D], preferred_element_type=F32).astype(BF16)


def score(lists, norms, t, queries):
    return lax.dot_general(lists[t], queries, (((1,), (1,)), ((), ())), preferred_element_type=F32) - norms[:, t : t + 1]


def sort_rows(scores):
    return exchange([scores[8 * i : 8 * i + 8] for i in range(TOPK)], SORT_PAIRS)


def score_kernel(*refs):
    groups, (lists, norms, out, chosen, best) = refs[:-5], refs[-5:]
    if len(groups) < 4:
        chosen[:, 32 * len(groups) :, :] = jnp.zeros((8, 128 - 32 * len(groups), D), BF16)
    for g, ref in enumerate(groups):
        picked = chosen_queries(ref[...])
        for t in range(8):
            chosen[t, 32 * g : 32 * g + 32, :] = picked[32 * t : 32 * t + 32]
    quads = []
    for quad in range(2):
        sets = [sort_rows(score(lists, norms, t, chosen[t])) for t in range(4 * quad, 4 * quad + 4)]
        quads.append(merged_rows(merged_rows(sets[0], sets[1], 1), merged_rows(sets[2], sets[3], 1), 2))
    for i, value in enumerate(merged_rows(quads[0], quads[1], 4)):
        best[8 * i : 8 * i + 8, :] = value
    for half in range(2):
        out[half] = jnp.concatenate([best[pl.ds(4 * half + t, TOPK, stride=8), :] for t in range(4)], 0).T


def last_kernel(lower, upper, lists, norms, first, second, out, best):
    picked = chosen_queries(jnp.concatenate([lower[...], upper[...]], 0))
    lane = lax.broadcasted_iota(jnp.int32, (256, 128), 1)
    sets = []
    for half in range(2):
        queries = picked[128 * half : 128 * half + 128]
        scores = score(lists, norms, 4 * half, queries)
        for t in range(1, 4):
            scores = jnp.where((lane >> 5) == t, score(lists, norms, 4 * half + t, queries), scores)
        sets.append(sort_rows(scores))
    values = merged_rows(sets[0], sets[1], 1)
    for shift in (2, 4):
        values = merged(values, [pltpu.roll(value, 8 - shift, 0) for value in values])
    for i, value in enumerate(values):
        best[8 * i : 8 * i + 8, :] = value
    own = own_group()
    for half in range(2):
        rows = best[pl.ds(half, TOPK, stride=8), :]
        turned = jnp.concatenate([rows] + [pltpu.roll(rows, 128 - 32 * t, 1) for t in range(1, 4)], 0).T
        found = [(mask, first[half, 32 * g : 32 * g + 32, :]) for g, mask in enumerate(FIRST_HALF)]
        found += [(mask, second[half, 32 * g : 32 * g + 32, :]) for g, mask in enumerate(SECOND_HALF)]
        for mask, values in found + [(7, turned[:32])]:
            place = (own ^ mask) * 8
            for b in range(8):
                out[place + b, 4 * half : 4 * half + 4, :] = values[4 * b : 4 * b + 4]


def final_kernel(back_ref, pick_ref, group_ref, out_ref, tiles, rows):
    pick = pick_ref[...]
    group = jnp.concatenate([group_ref[...]] * 4, 0)
    for z in range(4):
        left = back_ref[:, z >> 1, :, z & 1].reshape(128, 128).T
        found = jnp.zeros((128, 256), F32)
        for _ in range(3):
            piece = left.astype(BF16)
            left = left - piece.astype(F32)
            found = found + jnp.dot(piece, pick, preferred_element_type=F32)
        scores = found[:32]
        for t in range(1, 4):
            scores = jnp.where(group == t, found[32 * t : 32 * t + 32], scores)
        for half in range(2):
            tiles[pl.ds(2 * z + half, TOPK, stride=8), :] = scores[:, 128 * half : 128 * half + 128]
    values = [tiles[8 * i : 8 * i + 8, :] for i in range(TOPK)]
    for axis, shift in ((0, 4), (0, 2), (0, 1), (1, 64), (1, 32)):
        values = merged(values, [pltpu.roll(value, shift, axis) for value in values])
    for i, value in enumerate(values):
        rows[i : i + 1, :] = value[:1]
    out_ref[...] = rows[...].T[:32]


def params():
    return pltpu.CompilerParams(vmem_limit_bytes=20 * 1024 * 1024)


def spaces(text):
    kinds = {"v": pltpu.VMEM, "s": pltpu.SMEM, "h": pltpu.HBM, "a": pl.ANY}
    return [pl.BlockSpec(memory_space=kinds[kind]) for kind in text]


def hop(value, mask):
    return lax.ppermute(value, AXES, [(device, far(device, mask, False)) for device in range(N_DEV)])


def per_device(queries, probes, list_slot, valid_rows, database):
    shape = jax.ShapeDtypeStruct
    slots = list_slot.reshape(1, 128)
    probes = probes.T
    wide = pl.pallas_call(
        widen_kernel, out_shape=shape((8, 32, WIDE), BF16), in_specs=spaces("vvv"), out_specs=spaces("v")[0], name="widen"
    )(queries, probes, slots)
    near = lax.all_to_all(wide, AXES, 0, 0, axis_index_groups=NEAR_GROUPS, tiled=True).reshape(256, WIDE)
    sibling = lax.ppermute(database, AXES, CORE_SWAP)
    sibling_valid = lax.ppermute(valid_rows, AXES, CORE_SWAP)
    near, sibling, sibling_valid = lax.optimization_barrier((near, sibling, sibling_valid))

    groups = {0: near}
    for mask in (1, 2, 4):
        groups[mask] = hop(near, mask)
    lists, norms = pl.pallas_call(
        lists_kernel, out_shape=(pltpu.VMEM((8, 256, D), BF16), pltpu.VMEM((256, 128), F32)), in_specs=spaces("havv"),
        out_specs=spaces("vv"), scratch_shapes=[pltpu.SemaphoreType.DMA((8,))], compiler_params=params(), name="lists",
    )(pltpu.with_memory_space_constraint(database, pltpu.HBM), sibling, valid_rows.reshape(1, 4), sibling_valid.reshape(1, 4))
    groups[4], lists, norms = lax.optimization_barrier((groups[4], lists, norms))
    for mask, source, step in ((3, 1, 2), (6, 2, 4), (5, 4, 1)):
        groups[mask] = hop(groups[source], step)

    def scored(masks, name):
        return pl.pallas_call(
            score_kernel, out_shape=shape((2, 128, 128), F32), in_specs=spaces("v" * (len(masks) + 2)), out_specs=spaces("v")[0],
            scratch_shapes=[pltpu.VMEM((8, 128, D), BF16), pltpu.VMEM((256, 128), F32)], compiler_params=params(), name=name,
        )(*[groups[mask] for mask in masks], lists, norms)

    first = scored(FIRST_HALF, "score_first")
    groups[5], first = lax.optimization_barrier((groups[5], first))
    last = [hop(groups[5][:128], 2), hop(groups[3][128:], 4)]
    second = scored(SECOND_HALF, "score_second")
    *last, second = lax.optimization_barrier((*last, second))
    blocks = pl.pallas_call(
        last_kernel, out_shape=shape((N_CORE, 8, 128), F32), in_specs=spaces("vvvvvv"), out_specs=spaces("v")[0],
        scratch_shapes=[pltpu.VMEM((256, 128), F32)], compiler_params=params(), name="score_last",
    )(*last, lists, norms, first, second)
    pick, group = pl.pallas_call(
        wanted_kernel, out_shape=(pltpu.VMEM((128, 256), BF16), pltpu.VMEM((8, 256), jnp.int32)), in_specs=spaces("vv"),
        out_specs=spaces("vv"), name="wanted",
    )(probes, slots)
    back = lax.all_to_all(blocks, AXES, 0, 0, axis_index_groups=CORE_GROUPS, tiled=True)
    return pl.pallas_call(
        final_kernel, out_shape=shape((32, TOPK), F32), in_specs=spaces("vvv"), out_specs=spaces("v")[0],
        scratch_shapes=[pltpu.VMEM((256, 128), F32), pltpu.VMEM((32, 128), F32)], compiler_params=params(), name="final",
    )(back.reshape(4, 2, 4, 2, 8, 128), pick, group)


def solution(mesh):
    in_specs = (P(AXES, None), P(AXES, None), P(), P("owner"), P("owner", "replica", None))
    return jax.shard_map(per_device, mesh=mesh, in_specs=in_specs, out_specs=P(AXES, None), check_vma=False)
```

```python
import jax
import jax.numpy as jnp
from jax import lax
from jax.experimental import pallas as pl
from jax.experimental.pallas import tpu as pltpu
from jax.sharding import PartitionSpec as P

D = 1024
WIDE = D + 128
TOPK = 32
AXES = ("owner", "replica")
N_DEV = 128
N_CORE = 64
BIG = 1e30
F32 = jnp.float32
BF16 = jnp.bfloat16

PAIRING = {"a": (1, 0, 3, 2), "b": (3, 2, 1, 0)}
DIMS_A = ("za", "ya", "xb")
DIMS_B = ("zb", "yb", "xa")


def moved(device, dim):
    z, core, x, y = device % 4, device // 4 % 2, device // 8 % 4, device // 32
    place = {"x": x, "y": y, "z": z}
    place[dim[0]] = PAIRING[dim[1]][place[dim[0]]]
    return ((place["y"] * 4 + place["x"]) * 2 + core) * 4 + place["z"]


def core_of(device):
    return device // 4 % 2


def dims_of(core, first):
    return DIMS_A if (core == 0) == first else DIMS_B


def far(device, mask, first):
    for bit, dim in enumerate(dims_of(core_of(device), first)):
        if mask >> bit & 1:
            device = moved(device, dim)
    return device


def at_address(core, address):
    return far(far(4 * core, address >> 3, False), address & 7, True)


CORE_GROUPS = [[at_address(core, address) for address in range(N_CORE)] for core in range(2)]
NEAR_GROUPS = [group[start : start + 8] for group in CORE_GROUPS for start in range(0, N_CORE, 8)]
CORE_SWAP = [(device, device ^ 4) for device in range(N_DEV)]
FIRST_HALF = (0, 1, 2, 4)
SECOND_HALF = (5, 3, 6)
SPLIT = 160


def pairing_bits(place, core, axis):
    low, high = (place ^ (place >> 1)) & 1, place >> 1
    low_first = jnp.equal(core, 0 if axis + "a" in DIMS_A else 1)
    return jnp.where(low_first, low, high), jnp.where(low_first, high, low)


def own_group():
    owner = lax.axis_index("owner")
    places = {"z": lax.axis_index("replica"), "y": owner >> 3, "x": (owner >> 1) & 3}
    z, y, x = [pairing_bits(place, owner & 1, axis)[1] for axis, place in places.items()]
    return z + 2 * y + 4 * x


def sort_pairs(count):
    pairs = []
    p = 1
    while p < count:
        k = p
        while k >= 1:
            for j in range(k % p, count - k, 2 * k):
                for i in range(min(k, count - j - k)):
                    if (i + j) // (p * 2) == (i + j + k) // (p * 2):
                        pairs.append((i + j, i + j + k))
            k //= 2
        p *= 2
    return pairs


SORT_PAIRS = sort_pairs(TOPK)
MERGE_PAIRS = [(i, i + d) for d in (16, 8, 4, 2, 1) for i in range(TOPK) if not i & d]


def exchange(values, pairs):
    values = list(values)
    for i, j in pairs:
        values[i], values[j] = jnp.maximum(values[i], values[j]), jnp.minimum(values[i], values[j])
    return values


def merged(first, second):
    return exchange([jnp.maximum(first[i], second[TOPK - 1 - i]) for i in range(TOPK)], MERGE_PAIRS)


def merged_rows(first, second, shift):
    row = lax.broadcasted_iota(jnp.int32, (8, 128), 0)
    odd = (row & shift) != 0
    here = [jnp.where(odd, b, a) for a, b in zip(first, second)]
    there = [pltpu.roll(jnp.where(odd, a, b), 8 - shift, 0) for a, b in zip(first, second)]
    return merged(here, there)


def place_matrix(slot_ref):
    core = lax.rem(lax.axis_index("owner"), 2)
    places = jnp.bitwise_xor(slot_ref[...], 4 * core)
    return (places == lax.broadcasted_iota(jnp.int32, (128, 128), 0)).astype(BF16)


def rank_table(probes_ref, place):
    lists = lax.broadcasted_iota(jnp.int32, (128, 32), 0)
    named = jnp.zeros((128, 32), F32)
    for j in range(8):
        named = jnp.where(probes_ref[j : j + 1, :] == lists, 1.0, named)
    probed = jnp.dot(place, named.astype(BF16), preferred_element_type=F32)
    before = lax.broadcasted_iota(jnp.int32, (32, 32), 0) < lax.broadcasted_iota(jnp.int32, (32, 32), 1)
    rank = jnp.dot(probed.astype(BF16), before.astype(BF16), preferred_element_type=F32)
    return jnp.where(probed > 0.5, rank, -1.0)


def widen_kernel(queries_ref, probes_ref, slot_ref, out_ref):
    table = rank_table(probes_ref, place_matrix(slot_ref)).T.astype(BF16)
    for copy in range(8):
        out_ref[copy, :, :D] = queries_ref[...]
        out_ref[copy, :, D:] = table


def wanted_kernel(probes_ref, slot_ref, pick_ref, group_ref):
    place = place_matrix(slot_ref)
    rank = rank_table(probes_ref, place)
    index = lax.broadcasted_iota(jnp.int32, (128, 32), 0)
    core = lax.axis_index("owner") & 1
    for j in range(8):
        placed = jnp.dot(place, (probes_ref[j : j + 1, :] == index).astype(BF16), preferred_element_type=F32)
        where = jnp.sum(placed * index.astype(F32), 0, keepdims=True).astype(jnp.int32)
        slot = jnp.sum(placed * rank, 0, keepdims=True).astype(jnp.int32)
        chip = where >> 3
        y_first, y_second = pairing_bits(chip >> 2, core, "y")
        x_first, x_second = pairing_bits(chip & 3, core, "x")
        row = (x_second * 8 + y_second * 4 + x_first * 2 + y_first) * 8 + (where & 4) + slot
        pick_ref[:, 32 * j : 32 * j + 32] = (index == row).astype(BF16)
        group_ref[:, 32 * j : 32 * j + 32] = jnp.broadcast_to(where & 3, (8, 32))


def lists_kernel(own, sibling, own_valid, sibling_valid, lists, norms, sems):
    copies = []
    for t in range(8):
        copies.append(pltpu.make_async_copy(own.at[t] if t < 4 else sibling.at[t - 4], lists.at[t], sems.at[t]))
        copies[t].start()
    row = lax.axis_index("replica") * 256 + lax.broadcasted_iota(jnp.int32, (256, 1), 0)
    lane = lax.broadcasted_iota(jnp.int32, (256, 128), 1)
    total = jnp.zeros((256, 128), F32)
    for t in (4, 5, 6, 7, 0, 1, 2, 3):
        copies[t].wait()
        rows = lists[t].astype(F32)
        valid = (own_valid if t < 4 else sibling_valid)[0:1, t % 4 : t % 4 + 1]
        norm = jnp.where(row < valid, 0.5 * jnp.sum(rows * rows, 1, keepdims=True), BIG)
        total = jnp.where(lane == t, norm, total)
    norms[...] = total


def chosen_queries(wide):
    chip = lax.axis_index("owner") // 2
    column = lax.broadcasted_iota(jnp.int32, (256, 128), 0)
    wanted = (lax.broadcasted_iota(jnp.int32, (256, 128), 1) == chip * 8 + (column >> 5)).astype(BF16)
    rank = lax.dot_general(wanted, wide[:, D:], (((1,), (1,)), ((), ())), preferred_element_type=F32)
    column = lax.broadcasted_iota(jnp.int32, (256, 256), 0)
    same_block = (lax.broadcasted_iota(jnp.int32, (256, 256), 1) >> 5) == ((column >> 2) & 7)
    pick = (same_block & (rank == (column & 3).astype(F32))).astype(BF16)
    return jnp.dot(pick, wide[:, :D], preferred_element_type=F32).astype(BF16)


def score(lists, norms, t, queries):
    return lax.dot_general(lists[t], queries, (((1,), (1,)), ((), ())), preferred_element_type=F32) - norms[:, t : t + 1]


def sort_rows(scores):
    return exchange([scores[8 * i : 8 * i + 8] for i in range(TOPK)], SORT_PAIRS)


def score_kernel(*refs):
    groups, (lists, norms, out, chosen, best) = refs[:-5], refs[-5:]
    if len(groups) < 4:
        chosen[:, 32 * len(groups) :, :] = jnp.zeros((8, 128 - 32 * len(groups), D), BF16)
    for g, ref in enumerate(groups):
        picked = chosen_queries(ref[...])
        for t in range(8):
            chosen[t, 32 * g : 32 * g + 32, :] = picked[32 * t : 32 * t + 32]
    quads = []
    for quad in range(2):
        sets = [sort_rows(score(lists, norms, t, chosen[t])) for t in range(4 * quad, 4 * quad + 4)]
        quads.append(merged_rows(merged_rows(sets[0], sets[1], 1), merged_rows(sets[2], sets[3], 1), 2))
    for i, value in enumerate(merged_rows(quads[0], quads[1], 4)):
        best[8 * i : 8 * i + 8, :] = value
    for half in range(2):
        out[half] = jnp.concatenate([best[pl.ds(4 * half + t, TOPK, stride=8), :] for t in range(4)], 0).T


def last_kernel(lower, upper, lists, norms, first, second, out, best):
    picked = chosen_queries(jnp.concatenate([lower[...], upper[...]], 0))
    lane = lax.broadcasted_iota(jnp.int32, (256, 128), 1)
    sets = []
    for half in range(2):
        queries = picked[128 * half : 128 * half + 128]
        scores = score(lists, norms, 4 * half, queries)
        for t in range(1, 4):
            scores = jnp.where((lane >> 5) == t, score(lists, norms, 4 * half + t, queries), scores)
        sets.append(sort_rows(scores))
    values = merged_rows(sets[0], sets[1], 1)
    for shift in (2, 4):
        values = merged(values, [pltpu.roll(value, 8 - shift, 0) for value in values])
    for i, value in enumerate(values):
        best[8 * i : 8 * i + 8, :] = value
    own = own_group()
    for half in range(2):
        rows = best[pl.ds(half, TOPK, stride=8), :]
        turned = jnp.concatenate([rows] + [pltpu.roll(rows, 128 - 32 * t, 1) for t in range(1, 4)], 0).T
        found = [(mask, first[half, 32 * g : 32 * g + 32, :]) for g, mask in enumerate(FIRST_HALF)]
        found += [(mask, second[half, 32 * g : 32 * g + 32, :]) for g, mask in enumerate(SECOND_HALF)]
        for mask, values in found + [(7, turned[:32])]:
            place = (own ^ mask) * 8
            for b in range(8):
                out[place + b, 4 * half : 4 * half + 4, :] = values[4 * b : 4 * b + 4]


def final_kernel(back_ref, pick_ref, group_ref, out_ref, tiles, rows):
    pick = pick_ref[...]
    group = jnp.concatenate([group_ref[...]] * 4, 0)
    for z in range(4):
        left = back_ref[:, z >> 1, :, z & 1].reshape(128, 128).T
        found = jnp.zeros((128, 256), F32)
        for _ in range(3):
            piece = left.astype(BF16)
            left = left - piece.astype(F32)
            found = found + jnp.dot(piece, pick, preferred_element_type=F32)
        scores = found[:32]
        for t in range(1, 4):
            scores = jnp.where(group == t, found[32 * t : 32 * t + 32], scores)
        for half in range(2):
            tiles[pl.ds(2 * z + half, TOPK, stride=8), :] = scores[:, 128 * half : 128 * half + 128]
    values = [tiles[8 * i : 8 * i + 8, :] for i in range(TOPK)]
    for axis, shift in ((0, 4), (0, 2), (0, 1), (1, 64), (1, 32)):
        values = merged(values, [pltpu.roll(value, shift, axis) for value in values])
    for i, value in enumerate(values):
        rows[i : i + 1, :] = value[:1]
    out_ref[...] = rows[...].T[:32]


def params():
    return pltpu.CompilerParams(vmem_limit_bytes=20 * 1024 * 1024)


def spaces(text):
    kinds = {"v": pltpu.VMEM, "s": pltpu.SMEM, "h": pltpu.HBM, "a": pl.ANY}
    return [pl.BlockSpec(memory_space=kinds[kind]) for kind in text]


def hop(value, mask):
    return lax.ppermute(value, AXES, [(device, far(device, mask, False)) for device in range(N_DEV)])


def per_device(queries, probes, list_slot, valid_rows, database):
    shape = jax.ShapeDtypeStruct
    slots = list_slot.reshape(1, 128)
    probes = probes.T
    wide = pl.pallas_call(
        widen_kernel, out_shape=shape((8, 32, WIDE), BF16), in_specs=spaces("vvv"), out_specs=spaces("v")[0], name="widen"
    )(queries, probes, slots)
    near = lax.all_to_all(wide, AXES, 0, 0, axis_index_groups=NEAR_GROUPS, tiled=True).reshape(256, WIDE)
    sibling = lax.ppermute(database, AXES, CORE_SWAP)
    pick, group = pl.pallas_call(
        wanted_kernel, out_shape=(pltpu.VMEM((128, 256), BF16), pltpu.VMEM((8, 256), jnp.int32)), in_specs=spaces("vv"),
        out_specs=spaces("vv"), name="wanted",
    )(probes, slots)
    near, valid_rows, pick, group = lax.optimization_barrier((near, valid_rows, pick, group))
    sibling_valid = lax.ppermute(valid_rows, AXES, CORE_SWAP)

    groups = {0: near}
    for mask in (1, 2, 4):
        groups[mask] = hop(near, mask)
    lists, norms = pl.pallas_call(
        lists_kernel, out_shape=(pltpu.VMEM((8, 256, D), BF16), pltpu.VMEM((256, 128), F32)), in_specs=spaces("havv"),
        out_specs=spaces("vv"), scratch_shapes=[pltpu.SemaphoreType.DMA((8,))], compiler_params=params(), name="lists",
    )(pltpu.with_memory_space_constraint(database, pltpu.HBM), sibling, valid_rows.reshape(1, 4), sibling_valid.reshape(1, 4))
    groups[4], lists, norms = lax.optimization_barrier((groups[4], lists, norms))
    for mask, source, step in ((3, 1, 2), (6, 2, 4), (5, 4, 1)):
        groups[mask] = hop(groups[source], step)

    def scored(masks, name):
        return pl.pallas_call(
            score_kernel, out_shape=shape((2, 128, 128), F32), in_specs=spaces("v" * (len(masks) + 2)), out_specs=spaces("v")[0],
            scratch_shapes=[pltpu.VMEM((8, 128, D), BF16), pltpu.VMEM((256, 128), F32)], compiler_params=params(), name=name,
        )(*[groups[mask] for mask in masks], lists, norms)

    first = scored(FIRST_HALF, "score_first")
    groups[5], first = lax.optimization_barrier((groups[5], first))
    last = [hop(groups[5][:SPLIT], 2), hop(groups[3][SPLIT:], 4)]
    second = scored(SECOND_HALF, "score_second")
    *last, second = lax.optimization_barrier((*last, second))
    blocks = pl.pallas_call(
        last_kernel, out_shape=shape((N_CORE, 8, 128), F32), in_specs=spaces("vvvvvv"), out_specs=spaces("v")[0],
        scratch_shapes=[pltpu.VMEM((256, 128), F32)], compiler_params=params(), name="score_last",
    )(*last, lists, norms, first, second)
    back = lax.all_to_all(blocks, AXES, 0, 0, axis_index_groups=CORE_GROUPS, tiled=True)
    return pl.pallas_call(
        final_kernel, out_shape=shape((32, TOPK), F32), in_specs=spaces("vvv"), out_specs=spaces("v")[0],
        scratch_shapes=[pltpu.VMEM((256, 128), F32), pltpu.VMEM((32, 128), F32)], compiler_params=params(), name="final",
    )(back.reshape(4, 2, 4, 2, 8, 128), pick, group)


def solution(mesh):
    in_specs = (P(AXES, None), P(AXES, None), P(), P("owner"), P("owner", "replica", None))
    return jax.shard_map(per_device, mesh=mesh, in_specs=in_specs, out_specs=P(AXES, None), check_vma=False)
```

```python
import jax
import jax.numpy as jnp
from jax import lax
from jax.experimental import pallas as pl
from jax.experimental.pallas import tpu as pltpu
from jax.sharding import PartitionSpec as P

D = 1024
WIDE = D + 128
TOPK = 32
AXES = ("owner", "replica")
N_DEV = 128
N_CORE = 64
BIG = 1e30
F32 = jnp.float32
BF16 = jnp.bfloat16

PAIRING = {"a": (1, 0, 3, 2), "b": (3, 2, 1, 0)}
DIMS_A = ("za", "ya", "xb")
DIMS_B = ("zb", "yb", "xa")


def moved(device, dim):
    z, core, x, y = device % 4, device // 4 % 2, device // 8 % 4, device // 32
    place = {"x": x, "y": y, "z": z}
    place[dim[0]] = PAIRING[dim[1]][place[dim[0]]]
    return ((place["y"] * 4 + place["x"]) * 2 + core) * 4 + place["z"]


def core_of(device):
    return device // 4 % 2


def dims_of(core, first):
    return DIMS_A if (core == 0) == first else DIMS_B


def far(device, mask, first):
    for bit, dim in enumerate(dims_of(core_of(device), first)):
        if mask >> bit & 1:
            device = moved(device, dim)
    return device


def at_address(core, address):
    return far(far(4 * core, address >> 3, False), address & 7, True)


CORE_GROUPS = [[at_address(core, address) for address in range(N_CORE)] for core in range(2)]
NEAR_GROUPS = [group[start : start + 8] for group in CORE_GROUPS for start in range(0, N_CORE, 8)]
CORE_SWAP = [(device, device ^ 4) for device in range(N_DEV)]
FIRST_HALF = (0, 1, 2, 4)
SECOND_HALF = (5, 3, 6)
SPLIT = 160


def pairing_bits(place, core, axis):
    low, high = (place ^ (place >> 1)) & 1, place >> 1
    low_first = jnp.equal(core, 0 if axis + "a" in DIMS_A else 1)
    return jnp.where(low_first, low, high), jnp.where(low_first, high, low)


def own_group():
    owner = lax.axis_index("owner")
    places = {"z": lax.axis_index("replica"), "y": owner >> 3, "x": (owner >> 1) & 3}
    z, y, x = [pairing_bits(place, owner & 1, axis)[1] for axis, place in places.items()]
    return z + 2 * y + 4 * x


def sort_pairs(count):
    pairs = []
    p = 1
    while p < count:
        k = p
        while k >= 1:
            for j in range(k % p, count - k, 2 * k):
                for i in range(min(k, count - j - k)):
                    if (i + j) // (p * 2) == (i + j + k) // (p * 2):
                        pairs.append((i + j, i + j + k))
            k //= 2
        p *= 2
    return pairs


SORT_PAIRS = sort_pairs(TOPK)
MERGE_PAIRS = [(i, i + d) for d in (16, 8, 4, 2, 1) for i in range(TOPK) if not i & d]


def exchange(values, pairs):
    values = list(values)
    for i, j in pairs:
        values[i], values[j] = jnp.maximum(values[i], values[j]), jnp.minimum(values[i], values[j])
    return values


def merged(first, second):
    return exchange([jnp.maximum(first[i], second[TOPK - 1 - i]) for i in range(TOPK)], MERGE_PAIRS)


def merged_rows(first, second, shift):
    row = lax.broadcasted_iota(jnp.int32, (8, 128), 0)
    odd = (row & shift) != 0
    here = [jnp.where(odd, b, a) for a, b in zip(first, second)]
    there = [pltpu.roll(jnp.where(odd, a, b), 8 - shift, 0) for a, b in zip(first, second)]
    return merged(here, there)


def place_matrix(slot_ref):
    core = lax.rem(lax.axis_index("owner"), 2)
    places = jnp.bitwise_xor(slot_ref[...], 4 * core)
    return (places == lax.broadcasted_iota(jnp.int32, (128, 128), 0)).astype(BF16)


def rank_table(probes_ref, place):
    lists = lax.broadcasted_iota(jnp.int32, (128, 32), 0)
    named = jnp.zeros((128, 32), F32)
    for j in range(8):
        named = jnp.where(probes_ref[j : j + 1, :] == lists, 1.0, named)
    probed = jnp.dot(place, named.astype(BF16), preferred_element_type=F32)
    before = lax.broadcasted_iota(jnp.int32, (32, 32), 0) < lax.broadcasted_iota(jnp.int32, (32, 32), 1)
    rank = jnp.dot(probed.astype(BF16), before.astype(BF16), preferred_element_type=F32)
    return jnp.where(probed > 0.5, rank, -1.0)


def widen_kernel(queries_ref, probes_ref, slot_ref, out_ref):
    table = rank_table(probes_ref, place_matrix(slot_ref)).T.astype(BF16)
    for copy in range(8):
        out_ref[copy, :, :D] = queries_ref[...]
        out_ref[copy, :, D:] = table


def find_wanted(probes_ref, slot_ref, pick_ref, group_ref):
    place = place_matrix(slot_ref)
    rank = rank_table(probes_ref, place)
    index = lax.broadcasted_iota(jnp.int32, (128, 32), 0)
    core = lax.axis_index("owner") & 1
    for j in range(8):
        placed = jnp.dot(place, (probes_ref[j : j + 1, :] == index).astype(BF16), preferred_element_type=F32)
        where = jnp.sum(placed * index.astype(F32), 0, keepdims=True).astype(jnp.int32)
        slot = jnp.sum(placed * rank, 0, keepdims=True).astype(jnp.int32)
        chip = where >> 3
        y_first, y_second = pairing_bits(chip >> 2, core, "y")
        x_first, x_second = pairing_bits(chip & 3, core, "x")
        row = (x_second * 8 + y_second * 4 + x_first * 2 + y_first) * 8 + (where & 4) + slot
        pick_ref[:, 32 * j : 32 * j + 32] = (index == row).astype(BF16)
        group_ref[:, 32 * j : 32 * j + 32] = jnp.broadcast_to(where & 3, (8, 32))


def lists_kernel(own, sibling, own_valid, sibling_valid, lists, norms, sems):
    copies = []
    for t in range(8):
        copies.append(pltpu.make_async_copy(own.at[t] if t < 4 else sibling.at[t - 4], lists.at[t], sems.at[t]))
        copies[t].start()
    row = lax.axis_index("replica") * 256 + lax.broadcasted_iota(jnp.int32, (256, 1), 0)
    lane = lax.broadcasted_iota(jnp.int32, (256, 128), 1)
    total = jnp.zeros((256, 128), F32)
    for t in (4, 5, 6, 7, 0, 1, 2, 3):
        copies[t].wait()
        rows = lists[t].astype(F32)
        valid = (own_valid if t < 4 else sibling_valid)[0:1, t % 4 : t % 4 + 1]
        norm = jnp.where(row < valid, 0.5 * jnp.sum(rows * rows, 1, keepdims=True), BIG)
        total = jnp.where(lane == t, norm, total)
    norms[...] = total


def chosen_queries(wide):
    chip = lax.axis_index("owner") // 2
    column = lax.broadcasted_iota(jnp.int32, (256, 128), 0)
    wanted = (lax.broadcasted_iota(jnp.int32, (256, 128), 1) == chip * 8 + (column >> 5)).astype(BF16)
    rank = lax.dot_general(wanted, wide[:, D:], (((1,), (1,)), ((), ())), preferred_element_type=F32)
    column = lax.broadcasted_iota(jnp.int32, (256, 256), 0)
    same_block = (lax.broadcasted_iota(jnp.int32, (256, 256), 1) >> 5) == ((column >> 2) & 7)
    pick = (same_block & (rank == (column & 3).astype(F32))).astype(BF16)
    return jnp.dot(pick, wide[:, :D], preferred_element_type=F32).astype(BF16)


def score(lists, norms, t, queries):
    return lax.dot_general(lists[t], queries, (((1,), (1,)), ((), ())), preferred_element_type=F32) - norms[:, t : t + 1]


def sort_rows(scores):
    return exchange([scores[8 * i : 8 * i + 8] for i in range(TOPK)], SORT_PAIRS)


def score_groups(groups, lists, norms, out, chosen, best):
    if len(groups) < 4:
        chosen[:, 32 * len(groups) :, :] = jnp.zeros((8, 128 - 32 * len(groups), D), BF16)
    for g, ref in enumerate(groups):
        picked = chosen_queries(ref[...])
        for t in range(8):
            chosen[t, 32 * g : 32 * g + 32, :] = picked[32 * t : 32 * t + 32]
    quads = []
    for quad in range(2):
        sets = [sort_rows(score(lists, norms, t, chosen[t])) for t in range(4 * quad, 4 * quad + 4)]
        quads.append(merged_rows(merged_rows(sets[0], sets[1], 1), merged_rows(sets[2], sets[3], 1), 2))
    for i, value in enumerate(merged_rows(quads[0], quads[1], 4)):
        best[8 * i : 8 * i + 8, :] = value
    for half in range(2):
        out[half] = jnp.concatenate([best[pl.ds(4 * half + t, TOPK, stride=8), :] for t in range(4)], 0).T


def first_kernel(*refs):
    score_groups(refs[:4], *refs[4:])


def second_kernel(*refs):
    groups, (lists, norms, probes, slots, out, pick, group, chosen, best) = refs[:3], refs[3:]
    score_groups(groups, lists, norms, out, chosen, best)
    find_wanted(probes, slots, pick, group)


def last_kernel(lower, upper, lists, norms, first, second, out, best):
    picked = chosen_queries(jnp.concatenate([lower[...], upper[...]], 0))
    lane = lax.broadcasted_iota(jnp.int32, (256, 128), 1)
    sets = []
    for half in range(2):
        queries = picked[128 * half : 128 * half + 128]
        scores = score(lists, norms, 4 * half, queries)
        for t in range(1, 4):
            scores = jnp.where((lane >> 5) == t, score(lists, norms, 4 * half + t, queries), scores)
        sets.append(sort_rows(scores))
    values = merged_rows(sets[0], sets[1], 1)
    for shift in (2, 4):
        values = merged(values, [pltpu.roll(value, 8 - shift, 0) for value in values])
    for i, value in enumerate(values):
        best[8 * i : 8 * i + 8, :] = value
    own = own_group()
    for half in range(2):
        rows = best[pl.ds(half, TOPK, stride=8), :]
        turned = jnp.concatenate([rows] + [pltpu.roll(rows, 128 - 32 * t, 1) for t in range(1, 4)], 0).T
        found = [(mask, first[half, 32 * g : 32 * g + 32, :]) for g, mask in enumerate(FIRST_HALF)]
        found += [(mask, second[half, 32 * g : 32 * g + 32, :]) for g, mask in enumerate(SECOND_HALF)]
        for mask, values in found + [(7, turned[:32])]:
            place = (own ^ mask) * 8
            for b in range(8):
                out[place + b, 4 * half : 4 * half + 4, :] = values[4 * b : 4 * b + 4]


def final_kernel(back_ref, pick_ref, group_ref, out_ref, tiles, rows):
    pick = pick_ref[...]
    group = jnp.concatenate([group_ref[...]] * 4, 0)
    for z in range(4):
        left = back_ref[:, z >> 1, :, z & 1].reshape(128, 128).T
        found = jnp.zeros((128, 256), F32)
        for _ in range(3):
            piece = left.astype(BF16)
            left = left - piece.astype(F32)
            found = found + jnp.dot(piece, pick, preferred_element_type=F32)
        scores = found[:32]
        for t in range(1, 4):
            scores = jnp.where(group == t, found[32 * t : 32 * t + 32], scores)
        for half in range(2):
            tiles[pl.ds(2 * z + half, TOPK, stride=8), :] = scores[:, 128 * half : 128 * half + 128]
    values = [tiles[8 * i : 8 * i + 8, :] for i in range(TOPK)]
    for axis, shift in ((0, 4), (0, 2), (0, 1), (1, 64), (1, 32)):
        values = merged(values, [pltpu.roll(value, shift, axis) for value in values])
    for i, value in enumerate(values):
        rows[i : i + 1, :] = value[:1]
    out_ref[...] = rows[...].T[:32]


def params():
    return pltpu.CompilerParams(vmem_limit_bytes=20 * 1024 * 1024)


def spaces(text):
    kinds = {"v": pltpu.VMEM, "s": pltpu.SMEM, "h": pltpu.HBM, "a": pl.ANY}
    return [pl.BlockSpec(memory_space=kinds[kind]) for kind in text]


def hop(value, mask):
    return lax.ppermute(value, AXES, [(device, far(device, mask, False)) for device in range(N_DEV)])


def per_device(queries, probes, list_slot, valid_rows, database):
    shape = jax.ShapeDtypeStruct
    slots = list_slot.reshape(1, 128)
    probes = probes.T
    wide = pl.pallas_call(
        widen_kernel, out_shape=pltpu.VMEM((8, 32, WIDE), BF16), in_specs=spaces("vvv"), out_specs=spaces("v")[0], name="widen"
    )(queries, probes, slots)
    near = lax.all_to_all(wide, AXES, 0, 0, axis_index_groups=NEAR_GROUPS, tiled=True).reshape(256, WIDE)
    sibling = lax.ppermute(database, AXES, CORE_SWAP)
    near, valid_rows = lax.optimization_barrier((near, valid_rows))
    sibling_valid = lax.ppermute(valid_rows, AXES, CORE_SWAP)

    groups = {0: near}
    for mask in (1, 2, 4):
        groups[mask] = hop(near, mask)
    lists, norms = pl.pallas_call(
        lists_kernel, out_shape=(pltpu.VMEM((8, 256, D), BF16), pltpu.VMEM((256, 128), F32)), in_specs=spaces("havv"),
        out_specs=spaces("vv"), scratch_shapes=[pltpu.SemaphoreType.DMA((8,))], compiler_params=params(), name="lists",
    )(pltpu.with_memory_space_constraint(database, pltpu.HBM), sibling, valid_rows.reshape(1, 4), sibling_valid.reshape(1, 4))
    groups[4], lists, norms = lax.optimization_barrier((groups[4], lists, norms))
    for mask, source, step in ((3, 1, 2), (6, 2, 4), (5, 4, 1)):
        groups[mask] = hop(groups[source], step)

    def scored(kernel, masks, more, out_shape, name):
        return pl.pallas_call(
            kernel, out_shape=out_shape, in_specs=spaces("v" * (len(masks) + 2 + len(more))), out_specs=spaces("v" * len(out_shape)),
            scratch_shapes=[pltpu.VMEM((8, 128, D), BF16), pltpu.VMEM((256, 128), F32)], compiler_params=params(), name=name,
        )(*[groups[mask] for mask in masks], lists, norms, *more)

    best_shape = pltpu.VMEM((2, 128, 128), F32)
    first, = scored(first_kernel, FIRST_HALF, (), (best_shape,), "score_first")
    groups[5], first = lax.optimization_barrier((groups[5], first))
    last = [hop(groups[5][:SPLIT], 2), hop(groups[3][SPLIT:], 4)]
    wanted_shapes = (pltpu.VMEM((128, 256), BF16), pltpu.VMEM((8, 256), jnp.int32))
    second, pick, group = scored(second_kernel, SECOND_HALF, (probes, slots), (best_shape, *wanted_shapes), "score_second")
    *last, second = lax.optimization_barrier((*last, second))
    blocks = pl.pallas_call(
        last_kernel, out_shape=shape((N_CORE, 8, 128), F32), in_specs=spaces("vvvvvv"), out_specs=spaces("v")[0],
        scratch_shapes=[pltpu.VMEM((256, 128), F32)], compiler_params=params(), name="score_last",
    )(*last, lists, norms, first, second)
    back = lax.all_to_all(blocks, AXES, 0, 0, axis_index_groups=CORE_GROUPS, tiled=True)
    return pl.pallas_call(
        final_kernel, out_shape=shape((32, TOPK), F32), in_specs=spaces("vvv"), out_specs=spaces("v")[0],
        scratch_shapes=[pltpu.VMEM((256, 128), F32), pltpu.VMEM((32, 128), F32)], compiler_params=params(), name="final",
    )(back.reshape(4, 2, 4, 2, 8, 128), pick, group)


def solution(mesh):
    in_specs = (P(AXES, None), P(AXES, None), P(), P("owner"), P("owner", "replica", None))
    return jax.shard_map(per_device, mesh=mesh, in_specs=in_specs, out_specs=P(AXES, None), check_vma=False)
```

```python
import jax
import jax.numpy as jnp
from jax import lax
from jax.experimental import pallas as pl
from jax.experimental.pallas import tpu as pltpu
from jax.sharding import PartitionSpec as P

D = 1024
WIDE = D + 128
TOPK = 32
AXES = ("owner", "replica")
N_DEV = 128
N_CORE = 64
BIG = 1e30
F32 = jnp.float32
BF16 = jnp.bfloat16

PAIRING = {"a": (1, 0, 3, 2), "b": (3, 2, 1, 0)}
DIMS_A = ("za", "ya", "xb")
DIMS_B = ("zb", "yb", "xa")


def moved(device, dim):
    z, core, x, y = device % 4, device // 4 % 2, device // 8 % 4, device // 32
    place = {"x": x, "y": y, "z": z}
    place[dim[0]] = PAIRING[dim[1]][place[dim[0]]]
    return ((place["y"] * 4 + place["x"]) * 2 + core) * 4 + place["z"]


def core_of(device):
    return device // 4 % 2


def dims_of(core, first):
    return DIMS_A if (core == 0) == first else DIMS_B


def far(device, mask, first):
    for bit, dim in enumerate(dims_of(core_of(device), first)):
        if mask >> bit & 1:
            device = moved(device, dim)
    return device


def at_address(core, address):
    return far(far(4 * core, address >> 3, False), address & 7, True)


CORE_GROUPS = [[at_address(core, address) for address in range(N_CORE)] for core in range(2)]
NEAR_GROUPS = [group[start : start + 8] for group in CORE_GROUPS for start in range(0, N_CORE, 8)]
CORE_SWAP = [(device, device ^ 4) for device in range(N_DEV)]
FIRST_HALF = (0, 1, 2, 4)
SECOND_HALF = (5, 3, 6)
SPLIT = 160


def pairing_bits(place, core, axis):
    low, high = (place ^ (place >> 1)) & 1, place >> 1
    low_first = jnp.equal(core, 0 if axis + "a" in DIMS_A else 1)
    return jnp.where(low_first, low, high), jnp.where(low_first, high, low)


def own_group():
    owner = lax.axis_index("owner")
    places = {"z": lax.axis_index("replica"), "y": owner >> 3, "x": (owner >> 1) & 3}
    z, y, x = [pairing_bits(place, owner & 1, axis)[1] for axis, place in places.items()]
    return z + 2 * y + 4 * x


def sort_pairs(count):
    pairs = []
    p = 1
    while p < count:
        k = p
        while k >= 1:
            for j in range(k % p, count - k, 2 * k):
                for i in range(min(k, count - j - k)):
                    if (i + j) // (p * 2) == (i + j + k) // (p * 2):
                        pairs.append((i + j, i + j + k))
            k //= 2
        p *= 2
    return pairs


SORT_PAIRS = sort_pairs(TOPK)
MERGE_PAIRS = [(i, i + d) for d in (16, 8, 4, 2, 1) for i in range(TOPK) if not i & d]


def exchange(values, pairs):
    values = list(values)
    for i, j in pairs:
        values[i], values[j] = jnp.maximum(values[i], values[j]), jnp.minimum(values[i], values[j])
    return values


def merged(first, second):
    return exchange([jnp.maximum(first[i], second[TOPK - 1 - i]) for i in range(TOPK)], MERGE_PAIRS)


def merged_rows(first, second, shift):
    row = lax.broadcasted_iota(jnp.int32, (8, 128), 0)
    odd = (row & shift) != 0
    here = [jnp.where(odd, b, a) for a, b in zip(first, second)]
    there = [pltpu.roll(jnp.where(odd, a, b), 8 - shift, 0) for a, b in zip(first, second)]
    return merged(here, there)


def place_matrix(slot_ref):
    core = lax.rem(lax.axis_index("owner"), 2)
    places = jnp.bitwise_xor(slot_ref[...], 4 * core)
    return (places == lax.broadcasted_iota(jnp.int32, (128, 128), 0)).astype(BF16)


def rank_table(probes_ref, place):
    lists = lax.broadcasted_iota(jnp.int32, (128, 32), 0)
    named = jnp.zeros((128, 32), F32)
    for j in range(8):
        named = jnp.where(probes_ref[j : j + 1, :] == lists, 1.0, named)
    probed = jnp.dot(place, named.astype(BF16), preferred_element_type=F32)
    before = lax.broadcasted_iota(jnp.int32, (32, 32), 0) < lax.broadcasted_iota(jnp.int32, (32, 32), 1)
    rank = jnp.dot(probed.astype(BF16), before.astype(BF16), preferred_element_type=F32)
    return jnp.where(probed > 0.5, rank, -1.0)


def widen_kernel(queries_ref, probes_ref, slot_ref, out_ref):
    table = rank_table(probes_ref, place_matrix(slot_ref)).T.astype(BF16)
    for copy in range(8):
        out_ref[copy, :, :D] = queries_ref[...]
        out_ref[copy, :, D:] = table


def find_wanted(probes_ref, slot_ref, pick_ref, group_ref):
    place = place_matrix(slot_ref)
    rank = rank_table(probes_ref, place)
    index = lax.broadcasted_iota(jnp.int32, (128, 32), 0)
    core = lax.axis_index("owner") & 1
    for j in range(8):
        placed = jnp.dot(place, (probes_ref[j : j + 1, :] == index).astype(BF16), preferred_element_type=F32)
        where = jnp.sum(placed * index.astype(F32), 0, keepdims=True).astype(jnp.int32)
        slot = jnp.sum(placed * rank, 0, keepdims=True).astype(jnp.int32)
        chip = where >> 3
        y_first, y_second = pairing_bits(chip >> 2, core, "y")
        x_first, x_second = pairing_bits(chip & 3, core, "x")
        row = (x_second * 8 + y_second * 4 + x_first * 2 + y_first) * 8 + (where & 4) + slot
        pick_ref[:, 32 * j : 32 * j + 32] = (index == row).astype(BF16)
        group_ref[:, 32 * j : 32 * j + 32] = jnp.broadcast_to(where & 3, (8, 32))


def lists_kernel(own, sibling, own_valid, sibling_valid, lists, norms, sems):
    copies = []
    for t in range(8):
        copies.append(pltpu.make_async_copy(own.at[t] if t < 4 else sibling.at[t - 4], lists.at[t], sems.at[t]))
        copies[t].start()
    row = lax.axis_index("replica") * 256 + lax.broadcasted_iota(jnp.int32, (256, 1), 0)
    lane = lax.broadcasted_iota(jnp.int32, (256, 128), 1)
    total = jnp.zeros((256, 128), F32)
    for t in (4, 5, 6, 7, 0, 1, 2, 3):
        copies[t].wait()
        rows = lists[t].astype(F32)
        valid = (own_valid if t < 4 else sibling_valid)[0:1, t % 4 : t % 4 + 1]
        norm = jnp.where(row < valid, 0.5 * jnp.sum(rows * rows, 1, keepdims=True), BIG)
        total = jnp.where(lane == t, norm, total)
    norms[...] = total


def chosen_queries(wide):
    chip = lax.axis_index("owner") // 2
    column = lax.broadcasted_iota(jnp.int32, (256, 128), 0)
    wanted = (lax.broadcasted_iota(jnp.int32, (256, 128), 1) == chip * 8 + (column >> 5)).astype(BF16)
    rank = lax.dot_general(wanted, wide[:, D:], (((1,), (1,)), ((), ())), preferred_element_type=F32)
    column = lax.broadcasted_iota(jnp.int32, (256, 256), 0)
    same_block = (lax.broadcasted_iota(jnp.int32, (256, 256), 1) >> 5) == ((column >> 2) & 7)
    pick = (same_block & (rank == (column & 3).astype(F32))).astype(BF16)
    return jnp.dot(pick, wide[:, :D], preferred_element_type=F32).astype(BF16)


def score(lists, norms, t, queries):
    return lax.dot_general(lists[t], queries, (((1,), (1,)), ((), ())), preferred_element_type=F32) - norms[:, t : t + 1]


def sort_rows(scores):
    return exchange([scores[8 * i : 8 * i + 8] for i in range(TOPK)], SORT_PAIRS)


def score_groups(groups, lists, norms, out, chosen, best):
    if len(groups) < 4:
        chosen[:, 32 * len(groups) :, :] = jnp.zeros((8, 128 - 32 * len(groups), D), BF16)
    for g, ref in enumerate(groups):
        picked = chosen_queries(ref[...])
        for t in range(8):
            chosen[t, 32 * g : 32 * g + 32, :] = picked[32 * t : 32 * t + 32]
    quads = []
    for quad in range(2):
        sets = [sort_rows(score(lists, norms, t, chosen[t])) for t in range(4 * quad, 4 * quad + 4)]
        quads.append(merged_rows(merged_rows(sets[0], sets[1], 1), merged_rows(sets[2], sets[3], 1), 2))
    for i, value in enumerate(merged_rows(quads[0], quads[1], 4)):
        best[8 * i : 8 * i + 8, :] = value
    for half in range(2):
        out[half] = jnp.concatenate([best[pl.ds(4 * half + t, TOPK, stride=8), :] for t in range(4)], 0).T


def first_kernel(*refs):
    score_groups(refs[:4], *refs[4:])


def second_kernel(*refs):
    groups, (lists, norms, probes, slots, out, pick, group, chosen, best) = refs[:3], refs[3:]
    score_groups(groups, lists, norms, out, chosen, best)
    find_wanted(probes, slots, pick, group)


def last_kernel(lower, upper, lists, norms, first, second, out, best):
    picked = chosen_queries(jnp.concatenate([lower[...], upper[...]], 0))
    lane = lax.broadcasted_iota(jnp.int32, (256, 128), 1)
    sets = []
    for half in range(2):
        queries = picked[128 * half : 128 * half + 128]
        scores = score(lists, norms, 4 * half, queries)
        for t in range(1, 4):
            scores = jnp.where((lane >> 5) == t, score(lists, norms, 4 * half + t, queries), scores)
        sets.append(sort_rows(scores))
    values = merged_rows(sets[0], sets[1], 1)
    for shift in (2, 4):
        values = merged(values, [pltpu.roll(value, 8 - shift, 0) for value in values])
    for i, value in enumerate(values):
        best[8 * i : 8 * i + 8, :] = value
    own = own_group()
    for half in range(2):
        rows = best[pl.ds(half, TOPK, stride=8), :]
        turned = jnp.concatenate([rows] + [pltpu.roll(rows, 128 - 32 * t, 1) for t in range(1, 4)], 0).T
        found = [(mask, first[half, 32 * g : 32 * g + 32, :]) for g, mask in enumerate(FIRST_HALF)]
        found += [(mask, second[half, 32 * g : 32 * g + 32, :]) for g, mask in enumerate(SECOND_HALF)]
        for mask, values in found + [(7, turned[:32])]:
            place = (own ^ mask) * 8
            for b in range(8):
                out[place + b, 4 * half : 4 * half + 4, :] = values[4 * b : 4 * b + 4]


def final_kernel(back_ref, pick_ref, group_ref, out_ref, tiles):
    pick = pick_ref[...]
    group = jnp.concatenate([group_ref[...]] * 4, 0)
    for z in range(4):
        left = back_ref[:, z >> 1, :, z & 1].reshape(128, 128).T
        found = jnp.zeros((128, 256), F32)
        for _ in range(3):
            piece = left.astype(BF16)
            left = left - piece.astype(F32)
            found = found + jnp.dot(piece, pick, preferred_element_type=F32)
        scores = found[:32]
        for t in range(1, 4):
            scores = jnp.where(group == t, found[32 * t : 32 * t + 32], scores)
        for half in range(2):
            tiles[pl.ds(2 * z + half, TOPK, stride=8), :] = scores[:, 128 * half : 128 * half + 128]
    values = [tiles[8 * i : 8 * i + 8, :] for i in range(TOPK)]
    for axis, shift in ((0, 4), (0, 2), (0, 1), (1, 64), (1, 32)):
        values = merged(values, [pltpu.roll(value, shift, axis) for value in values])
    row = lax.broadcasted_iota(jnp.int32, (8, 128), 0)
    ranked = []
    for first in range(0, TOPK, 8):
        rows = values[first]
        for i in range(1, 8):
            rows = jnp.where(row == i, values[first + i], rows)
        ranked.append(rows)
    out_ref[...] = jnp.concatenate(ranked, 0).T[:32]


def params():
    return pltpu.CompilerParams(vmem_limit_bytes=20 * 1024 * 1024)


def spaces(text):
    kinds = {"v": pltpu.VMEM, "s": pltpu.SMEM, "h": pltpu.HBM, "a": pl.ANY}
    return [pl.BlockSpec(memory_space=kinds[kind]) for kind in text]


def hop(value, mask):
    return lax.ppermute(value, AXES, [(device, far(device, mask, False)) for device in range(N_DEV)])


def per_device(queries, probes, list_slot, valid_rows, database):
    shape = jax.ShapeDtypeStruct
    slots = list_slot.reshape(1, 128)
    probes = probes.T
    wide = pl.pallas_call(
        widen_kernel, out_shape=pltpu.VMEM((8, 32, WIDE), BF16), in_specs=spaces("vvv"), out_specs=spaces("v")[0], name="widen"
    )(queries, probes, slots)
    near = lax.all_to_all(wide, AXES, 0, 0, axis_index_groups=NEAR_GROUPS, tiled=True).reshape(256, WIDE)
    sibling = lax.ppermute(database, AXES, CORE_SWAP)
    near, valid_rows = lax.optimization_barrier((near, valid_rows))
    sibling_valid = lax.ppermute(valid_rows, AXES, CORE_SWAP)

    groups = {0: near}
    for mask in (1, 2, 4):
        groups[mask] = hop(near, mask)
    lists, norms = pl.pallas_call(
        lists_kernel, out_shape=(pltpu.VMEM((8, 256, D), BF16), pltpu.VMEM((256, 128), F32)), in_specs=spaces("havv"),
        out_specs=spaces("vv"), scratch_shapes=[pltpu.SemaphoreType.DMA((8,))], compiler_params=params(), name="lists",
    )(pltpu.with_memory_space_constraint(database, pltpu.HBM), sibling, valid_rows.reshape(1, 4), sibling_valid.reshape(1, 4))
    groups[4], lists, norms = lax.optimization_barrier((groups[4], lists, norms))
    for mask, source, step in ((3, 1, 2), (6, 2, 4), (5, 4, 1)):
        groups[mask] = hop(groups[source], step)

    def scored(kernel, masks, more, out_shape, name):
        return pl.pallas_call(
            kernel, out_shape=out_shape, in_specs=spaces("v" * (len(masks) + 2 + len(more))), out_specs=spaces("v" * len(out_shape)),
            scratch_shapes=[pltpu.VMEM((8, 128, D), BF16), pltpu.VMEM((264, 128), F32)], compiler_params=params(), name=name,
        )(*[groups[mask] for mask in masks], lists, norms, *more)

    best_shape = pltpu.VMEM((2, 128, 128), F32)
    first, = scored(first_kernel, FIRST_HALF, (), (best_shape,), "score_first")
    groups[5], first = lax.optimization_barrier((groups[5], first))
    last = [hop(groups[5][:SPLIT], 2), hop(groups[3][SPLIT:], 4)]
    wanted_shapes = (pltpu.VMEM((128, 256), BF16), pltpu.VMEM((8, 256), jnp.int32))
    second, pick, group = scored(second_kernel, SECOND_HALF, (probes, slots), (best_shape, *wanted_shapes), "score_second")
    *last, second = lax.optimization_barrier((*last, second))
    blocks = pl.pallas_call(
        last_kernel, out_shape=shape((N_CORE, 8, 128), F32), in_specs=spaces("vvvvvv"), out_specs=spaces("v")[0],
        scratch_shapes=[pltpu.VMEM((264, 128), F32)], compiler_params=params(), name="score_last",
    )(*last, lists, norms, first, second)
    back = lax.all_to_all(blocks, AXES, 0, 0, axis_index_groups=CORE_GROUPS, tiled=True)
    return pl.pallas_call(
        final_kernel, out_shape=shape((32, TOPK), F32), in_specs=spaces("vvv"), out_specs=spaces("v")[0],
        scratch_shapes=[pltpu.VMEM((264, 128), F32)], compiler_params=params(), name="final",
    )(back.reshape(4, 2, 4, 2, 8, 128), pick, group)


def solution(mesh):
    in_specs = (P(AXES, None), P(AXES, None), P(), P("owner"), P("owner", "replica", None))
    return jax.shard_map(per_device, mesh=mesh, in_specs=in_specs, out_specs=P(AXES, None), check_vma=False)
```

```python
import jax
import jax.numpy as jnp
from jax import lax
from jax.experimental import pallas as pl
from jax.experimental.pallas import tpu as pltpu
from jax.sharding import PartitionSpec as P

D = 1024
WIDE = D + 128
TOPK = 32
AXES = ("owner", "replica")
N_DEV = 128
N_CORE = 64
BIG = 1e30
F32 = jnp.float32
BF16 = jnp.bfloat16

PAIRING = {"a": (1, 0, 3, 2), "b": (3, 2, 1, 0)}
DIMS_A = ("za", "ya", "xb")
DIMS_B = ("zb", "yb", "xa")


def moved(device, dim):
    z, core, x, y = device % 4, device // 4 % 2, device // 8 % 4, device // 32
    place = {"x": x, "y": y, "z": z}
    place[dim[0]] = PAIRING[dim[1]][place[dim[0]]]
    return ((place["y"] * 4 + place["x"]) * 2 + core) * 4 + place["z"]


def core_of(device):
    return device // 4 % 2


def dims_of(core, first):
    return DIMS_A if (core == 0) == first else DIMS_B


def far(device, mask, first):
    for bit, dim in enumerate(dims_of(core_of(device), first)):
        if mask >> bit & 1:
            device = moved(device, dim)
    return device


def at_address(core, address):
    return far(far(4 * core, address >> 3, False), address & 7, True)


CORE_GROUPS = [[at_address(core, address) for address in range(N_CORE)] for core in range(2)]
NEAR_GROUPS = [group[start : start + 8] for group in CORE_GROUPS for start in range(0, N_CORE, 8)]
CORE_SWAP = [(device, device ^ 4) for device in range(N_DEV)]
FIRST_HALF = (0, 1, 2, 4)
SECOND_HALF = (5, 3, 6)
SPLIT = 160


def pairing_bits(place, core, axis):
    low, high = (place ^ (place >> 1)) & 1, place >> 1
    low_first = jnp.equal(core, 0 if axis + "a" in DIMS_A else 1)
    return jnp.where(low_first, low, high), jnp.where(low_first, high, low)


def own_group():
    owner = lax.axis_index("owner")
    places = {"z": lax.axis_index("replica"), "y": owner >> 3, "x": (owner >> 1) & 3}
    z, y, x = [pairing_bits(place, owner & 1, axis)[1] for axis, place in places.items()]
    return z + 2 * y + 4 * x


def sort_pairs(count):
    pairs = []
    p = 1
    while p < count:
        k = p
        while k >= 1:
            for j in range(k % p, count - k, 2 * k):
                for i in range(min(k, count - j - k)):
                    if (i + j) // (p * 2) == (i + j + k) // (p * 2):
                        pairs.append((i + j, i + j + k))
            k //= 2
        p *= 2
    return pairs


SORT_PAIRS = sort_pairs(TOPK)
MERGE_PAIRS = [(i, i + d) for d in (16, 8, 4, 2, 1) for i in range(TOPK) if not i & d]


def exchange(values, pairs):
    values = list(values)
    for i, j in pairs:
        values[i], values[j] = jnp.maximum(values[i], values[j]), jnp.minimum(values[i], values[j])
    return values


def merged(first, second):
    return exchange([jnp.maximum(first[i], second[TOPK - 1 - i]) for i in range(TOPK)], MERGE_PAIRS)


def merged_rows(first, second, shift):
    row = lax.broadcasted_iota(jnp.int32, (8, 128), 0)
    odd = (row & shift) != 0
    here = [jnp.where(odd, b, a) for a, b in zip(first, second)]
    there = [pltpu.roll(jnp.where(odd, a, b), 8 - shift, 0) for a, b in zip(first, second)]
    return merged(here, there)


def place_matrix(slot_ref):
    core = lax.rem(lax.axis_index("owner"), 2)
    places = jnp.bitwise_xor(slot_ref[...], 4 * core)
    return (places == lax.broadcasted_iota(jnp.int32, (128, 128), 0)).astype(BF16)


def rank_table(probes_ref, place):
    lists = lax.broadcasted_iota(jnp.int32, (128, 32), 0)
    named = jnp.zeros((128, 32), F32)
    for j in range(8):
        named = jnp.where(probes_ref[j : j + 1, :] == lists, 1.0, named)
    probed = jnp.dot(place, named.astype(BF16), preferred_element_type=F32)
    before = lax.broadcasted_iota(jnp.int32, (32, 32), 0) < lax.broadcasted_iota(jnp.int32, (32, 32), 1)
    rank = jnp.dot(probed.astype(BF16), before.astype(BF16), preferred_element_type=F32)
    return jnp.where(probed > 0.5, rank, -1.0)


def widen_kernel(queries_ref, probes_ref, slot_ref, out_ref):
    table = rank_table(probes_ref, place_matrix(slot_ref)).T.astype(BF16)
    for copy in range(8):
        out_ref[copy, :, :D] = queries_ref[...]
        out_ref[copy, :, D:] = table


def find_wanted(probes_ref, slot_ref, pick_ref, group_ref):
    place = place_matrix(slot_ref)
    rank = rank_table(probes_ref, place)
    index = lax.broadcasted_iota(jnp.int32, (128, 32), 0)
    core = lax.axis_index("owner") & 1
    for j in range(8):
        placed = jnp.dot(place, (probes_ref[j : j + 1, :] == index).astype(BF16), preferred_element_type=F32)
        where = jnp.sum(placed * index.astype(F32), 0, keepdims=True).astype(jnp.int32)
        slot = jnp.sum(placed * rank, 0, keepdims=True).astype(jnp.int32)
        chip = where >> 3
        y_first, y_second = pairing_bits(chip >> 2, core, "y")
        x_first, x_second = pairing_bits(chip & 3, core, "x")
        row = (x_second * 8 + y_second * 4 + x_first * 2 + y_first) * 8 + (where & 4) + slot
        pick_ref[:, 32 * j : 32 * j + 32] = (index == row).astype(BF16)
        group_ref[:, 32 * j : 32 * j + 32] = jnp.broadcast_to(where & 3, (8, 32))


def lists_kernel(own, sibling, own_rows, sibling_valid, lists, norms, own_valid, sems):
    copies = []
    for t in range(8):
        copies.append(pltpu.make_async_copy(own.at[t] if t < 4 else sibling.at[t - 4], lists.at[t], sems.at[t]))
        copies[t].start()
    valid_copy = pltpu.make_async_copy(own_rows, own_valid, sems.at[8])
    valid_copy.start()
    row = lax.axis_index("replica") * 256 + lax.broadcasted_iota(jnp.int32, (256, 1), 0)
    lane = lax.broadcasted_iota(jnp.int32, (256, 128), 1)
    total = jnp.zeros((256, 128), F32)
    for t in (4, 5, 6, 7, 0, 1, 2, 3):
        if t == 0:
            valid_copy.wait()
        copies[t].wait()
        rows = lists[t].astype(F32)
        valid = (own_valid if t < 4 else sibling_valid)[0:1, t % 4 : t % 4 + 1]
        norm = jnp.where(row < valid, 0.5 * jnp.sum(rows * rows, 1, keepdims=True), BIG)
        total = jnp.where(lane == t, norm, total)
    norms[...] = total


def chosen_queries(wide):
    chip = lax.axis_index("owner") // 2
    column = lax.broadcasted_iota(jnp.int32, (256, 128), 0)
    wanted = (lax.broadcasted_iota(jnp.int32, (256, 128), 1) == chip * 8 + (column >> 5)).astype(BF16)
    rank = lax.dot_general(wanted, wide[:, D:], (((1,), (1,)), ((), ())), preferred_element_type=F32)
    column = lax.broadcasted_iota(jnp.int32, (256, 256), 0)
    same_block = (lax.broadcasted_iota(jnp.int32, (256, 256), 1) >> 5) == ((column >> 2) & 7)
    pick = (same_block & (rank == (column & 3).astype(F32))).astype(BF16)
    return jnp.dot(pick, wide[:, :D], preferred_element_type=F32).astype(BF16)


def score(lists, norms, t, queries):
    return lax.dot_general(lists[t], queries, (((1,), (1,)), ((), ())), preferred_element_type=F32) - norms[:, t : t + 1]


def sort_rows(scores):
    return exchange([scores[8 * i : 8 * i + 8] for i in range(TOPK)], SORT_PAIRS)


def score_groups(groups, lists, norms, out, chosen, best):
    if len(groups) < 4:
        chosen[:, 32 * len(groups) :, :] = jnp.zeros((8, 128 - 32 * len(groups), D), BF16)
    for g, ref in enumerate(groups):
        picked = chosen_queries(ref[...])
        for t in range(8):
            chosen[t, 32 * g : 32 * g + 32, :] = picked[32 * t : 32 * t + 32]
    quads = []
    for quad in range(2):
        sets = [sort_rows(score(lists, norms, t, chosen[t])) for t in range(4 * quad, 4 * quad + 4)]
        quads.append(merged_rows(merged_rows(sets[0], sets[1], 1), merged_rows(sets[2], sets[3], 1), 2))
    for i, value in enumerate(merged_rows(quads[0], quads[1], 4)):
        best[8 * i : 8 * i + 8, :] = value
    for half in range(2):
        out[half] = jnp.concatenate([best[pl.ds(4 * half + t, TOPK, stride=8), :] for t in range(4)], 0).T


def first_kernel(*refs):
    score_groups(refs[:4], *refs[4:])


def second_kernel(*refs):
    groups, (lists, norms, probes, slots, out, pick, group, chosen, best) = refs[:3], refs[3:]
    score_groups(groups, lists, norms, out, chosen, best)
    find_wanted(probes, slots, pick, group)


def last_kernel(lower, upper, lists, norms, first, second, out, best):
    picked = chosen_queries(jnp.concatenate([lower[...], upper[...]], 0))
    lane = lax.broadcasted_iota(jnp.int32, (256, 128), 1)
    sets = []
    for half in range(2):
        four = lists[4 * half : 4 * half + 4].reshape(1024, D)
        queries = picked[128 * half : 128 * half + 128]
        dots = lax.dot_general(four, queries, (((1,), (1,)), ((), ())), preferred_element_type=F32)
        scores = dots[:256] - norms[:, 4 * half : 4 * half + 1]
        for t in range(1, 4):
            other = dots[256 * t : 256 * t + 256] - norms[:, 4 * half + t : 4 * half + t + 1]
            scores = jnp.where((lane >> 5) == t, other, scores)
        sets.append(sort_rows(scores))
    values = merged_rows(sets[0], sets[1], 1)
    for shift in (2, 4):
        values = merged(values, [pltpu.roll(value, 8 - shift, 0) for value in values])
    for i, value in enumerate(values):
        best[8 * i : 8 * i + 8, :] = value
    own = own_group()
    for half in range(2):
        rows = best[pl.ds(half, TOPK, stride=8), :]
        turned = jnp.concatenate([rows] + [pltpu.roll(rows, 128 - 32 * t, 1) for t in range(1, 4)], 0).T
        found = [(mask, first[half, 32 * g : 32 * g + 32, :]) for g, mask in enumerate(FIRST_HALF)]
        found += [(mask, second[half, 32 * g : 32 * g + 32, :]) for g, mask in enumerate(SECOND_HALF)]
        for mask, values in found + [(7, turned[:32])]:
            place = (own ^ mask) * 8
            for b in range(8):
                out[place + b, 4 * half : 4 * half + 4, :] = values[4 * b : 4 * b + 4]


def final_kernel(back_ref, pick_ref, group_ref, out_ref, tiles):
    pick = pick_ref[...]
    group = jnp.concatenate([group_ref[...]] * 4, 0)
    pieces = []
    for z in range(4):
        left = back_ref[:, z >> 1, :, z & 1].reshape(128, 128).T
        for _ in range(3):
            pieces.append(left.astype(BF16))
            left = left - pieces[-1].astype(F32)
    products = jnp.dot(jnp.concatenate(pieces, 0), pick, preferred_element_type=F32)
    for z in range(4):
        high, middle, low = [products[128 * i : 128 * i + 128] for i in range(3 * z, 3 * z + 3)]
        found = high + middle + low
        scores = found[:32]
        for t in range(1, 4):
            scores = jnp.where(group == t, found[32 * t : 32 * t + 32], scores)
        for half in range(2):
            tiles[pl.ds(2 * z + half, TOPK, stride=8), :] = scores[:, 128 * half : 128 * half + 128]
    values = [tiles[8 * i : 8 * i + 8, :] for i in range(TOPK)]
    for axis, shift in ((0, 4), (0, 2), (0, 1), (1, 64), (1, 32)):
        values = merged(values, [pltpu.roll(value, shift, axis) for value in values])
    row = lax.broadcasted_iota(jnp.int32, (8, 128), 0)
    ranked = []
    for first in range(0, TOPK, 8):
        rows = values[first]
        for i in range(1, 8):
            rows = jnp.where(row == i, values[first + i], rows)
        ranked.append(rows)
    out_ref[...] = jnp.concatenate(ranked, 0).T[:32]


def params():
    return pltpu.CompilerParams(vmem_limit_bytes=20 * 1024 * 1024)


def spaces(text):
    kinds = {"v": pltpu.VMEM, "s": pltpu.SMEM, "h": pltpu.HBM, "a": pl.ANY}
    return [pl.BlockSpec(memory_space=kinds[kind]) for kind in text]


def hop(value, mask):
    return lax.ppermute(value, AXES, [(device, far(device, mask, False)) for device in range(N_DEV)])


def per_device(queries, probes, list_slot, valid_rows, database):
    shape = jax.ShapeDtypeStruct
    slots = list_slot.reshape(1, 128)
    probes = probes.T
    wide = pl.pallas_call(
        widen_kernel, out_shape=pltpu.VMEM((8, 32, WIDE), BF16), in_specs=spaces("vvv"), out_specs=spaces("v")[0], name="widen"
    )(queries, probes, slots)
    near = lax.all_to_all(wide, AXES, 0, 0, axis_index_groups=NEAR_GROUPS, tiled=True).reshape(256, WIDE)
    sibling = lax.ppermute(database, AXES, CORE_SWAP)
    near, valid_rows = lax.optimization_barrier((near, valid_rows))
    sibling_valid = lax.ppermute(valid_rows, AXES, CORE_SWAP)

    groups = {0: near}
    for mask in (1, 2, 4):
        groups[mask] = hop(near, mask)
    lists, norms = pl.pallas_call(
        lists_kernel, out_shape=(pltpu.VMEM((8, 256, D), BF16), pltpu.VMEM((256, 128), F32)), in_specs=spaces("hahv"),
        out_specs=spaces("vv"), scratch_shapes=[pltpu.VMEM((1, 4), jnp.int32), pltpu.SemaphoreType.DMA((9,))], compiler_params=params(), name="lists",
    )(pltpu.with_memory_space_constraint(database, pltpu.HBM), sibling, pltpu.with_memory_space_constraint(valid_rows.reshape(1, 4), pltpu.HBM), sibling_valid.reshape(1, 4))
    groups[4], lists, norms = lax.optimization_barrier((groups[4], lists, norms))
    for mask, source, step in ((3, 1, 2), (6, 2, 4), (5, 4, 1)):
        groups[mask] = hop(groups[source], step)

    def scored(kernel, masks, more, out_shape, name):
        return pl.pallas_call(
            kernel, out_shape=out_shape, in_specs=spaces("v" * (len(masks) + 2 + len(more))), out_specs=spaces("v" * len(out_shape)),
            scratch_shapes=[pltpu.VMEM((8, 128, D), BF16), pltpu.VMEM((264, 128), F32)], compiler_params=params(), name=name,
        )(*[groups[mask] for mask in masks], lists, norms, *more)

    best_shape = pltpu.VMEM((2, 128, 128), F32)
    first, = scored(first_kernel, FIRST_HALF, (), (best_shape,), "score_first")
    groups[5], first = lax.optimization_barrier((groups[5], first))
    last = [hop(groups[5][:SPLIT], 2), hop(groups[3][SPLIT:], 4)]
    wanted_shapes = (pltpu.VMEM((128, 256), BF16), pltpu.VMEM((8, 256), jnp.int32))
    second, pick, group = scored(second_kernel, SECOND_HALF, (probes, slots), (best_shape, *wanted_shapes), "score_second")
    *last, second = lax.optimization_barrier((*last, second))
    blocks = pl.pallas_call(
        last_kernel, out_shape=shape((N_CORE, 8, 128), F32), in_specs=spaces("vvvvvv"), out_specs=spaces("v")[0],
        scratch_shapes=[pltpu.VMEM((264, 128), F32)], compiler_params=params(), name="score_last",
    )(*last, lists, norms, first, second)
    back = lax.all_to_all(blocks, AXES, 0, 0, axis_index_groups=CORE_GROUPS, tiled=True)
    return pl.pallas_call(
        final_kernel, out_shape=shape((32, TOPK), F32), in_specs=spaces("vvv"), out_specs=spaces("v")[0],
        scratch_shapes=[pltpu.VMEM((264, 128), F32)], compiler_params=params(), name="final",
    )(back.reshape(4, 2, 4, 2, 8, 128), pick, group)


def solution(mesh):
    in_specs = (P(AXES, None), P(AXES, None), P(), P("owner"), P("owner", "replica", None))
    return jax.shard_map(per_device, mesh=mesh, in_specs=in_specs, out_specs=P(AXES, None), check_vma=False)
```

```python
import jax
import jax.numpy as jnp
from jax import lax
from jax.experimental import pallas as pl
from jax.experimental.pallas import tpu as pltpu
from jax.sharding import PartitionSpec as P

D = 1024
WIDE = D + 128
TOPK = 32
AXES = ("owner", "replica")
N_DEV = 128
N_CORE = 64
BIG = 1e30
F32 = jnp.float32
BF16 = jnp.bfloat16

PAIRING = {"a": (1, 0, 3, 2), "b": (3, 2, 1, 0)}
DIMS_A = ("za", "ya", "xb")
DIMS_B = ("zb", "yb", "xa")


def moved(device, dim):
    z, core, x, y = device % 4, device // 4 % 2, device // 8 % 4, device // 32
    place = {"x": x, "y": y, "z": z}
    place[dim[0]] = PAIRING[dim[1]][place[dim[0]]]
    return ((place["y"] * 4 + place["x"]) * 2 + core) * 4 + place["z"]


def core_of(device):
    return device // 4 % 2


def dims_of(core, first):
    return DIMS_A if (core == 0) == first else DIMS_B


def far(device, mask, first):
    for bit, dim in enumerate(dims_of(core_of(device), first)):
        if mask >> bit & 1:
            device = moved(device, dim)
    return device


def at_address(core, address):
    return far(far(4 * core, address >> 3, False), address & 7, True)


CORE_GROUPS = [[at_address(core, address) for address in range(N_CORE)] for core in range(2)]
NEAR_GROUPS = [group[start : start + 8] for group in CORE_GROUPS for start in range(0, N_CORE, 8)]
CORE_SWAP = [(device, device ^ 4) for device in range(N_DEV)]
FIRST_HALF = (0, 1, 2, 4)
SECOND_HALF = (5, 3, 6)
SPLIT = 160


def pairing_bits(place, core, axis):
    low, high = (place ^ (place >> 1)) & 1, place >> 1
    low_first = jnp.equal(core, 0 if axis + "a" in DIMS_A else 1)
    return jnp.where(low_first, low, high), jnp.where(low_first, high, low)


def own_group():
    owner = lax.axis_index("owner")
    places = {"z": lax.axis_index("replica"), "y": owner >> 3, "x": (owner >> 1) & 3}
    z, y, x = [pairing_bits(place, owner & 1, axis)[1] for axis, place in places.items()]
    return z + 2 * y + 4 * x


def sort_pairs(count):
    pairs = []
    p = 1
    while p < count:
        k = p
        while k >= 1:
            for j in range(k % p, count - k, 2 * k):
                for i in range(min(k, count - j - k)):
                    if (i + j) // (p * 2) == (i + j + k) // (p * 2):
                        pairs.append((i + j, i + j + k))
            k //= 2
        p *= 2
    return pairs


SORT_PAIRS = sort_pairs(TOPK)
MERGE_PAIRS = [(i, i + d) for d in (16, 8, 4, 2, 1) for i in range(TOPK) if not i & d]


def exchange(values, pairs):
    values = list(values)
    for i, j in pairs:
        values[i], values[j] = jnp.maximum(values[i], values[j]), jnp.minimum(values[i], values[j])
    return values


def merged(first, second):
    return exchange([jnp.maximum(first[i], second[TOPK - 1 - i]) for i in range(TOPK)], MERGE_PAIRS)


def merged_rows(first, second, shift):
    row = lax.broadcasted_iota(jnp.int32, (8, 128), 0)
    odd = (row & shift) != 0
    here = [jnp.where(odd, b, a) for a, b in zip(first, second)]
    there = [pltpu.roll(jnp.where(odd, a, b), 8 - shift, 0) for a, b in zip(first, second)]
    return merged(here, there)


def place_matrix(slot_ref):
    core = lax.rem(lax.axis_index("owner"), 2)
    places = jnp.bitwise_xor(slot_ref[...], 4 * core)
    return (places == lax.broadcasted_iota(jnp.int32, (128, 128), 0)).astype(BF16)


def rank_table(probes_ref, place):
    lists = lax.broadcasted_iota(jnp.int32, (128, 32), 0)
    named = jnp.zeros((128, 32), F32)
    for j in range(8):
        named = jnp.where(probes_ref[j : j + 1, :] == lists, 1.0, named)
    probed = jnp.dot(place, named.astype(BF16), preferred_element_type=F32)
    before = lax.broadcasted_iota(jnp.int32, (32, 32), 0) < lax.broadcasted_iota(jnp.int32, (32, 32), 1)
    rank = jnp.dot(probed.astype(BF16), before.astype(BF16), preferred_element_type=F32)
    return jnp.where(probed > 0.5, rank, -1.0)


def widen_kernel(queries_ref, probes_ref, slot_ref, out_ref):
    lists = lax.broadcasted_iota(jnp.int32, (128, 32), 0)
    named = jnp.zeros((128, 32), F32)
    for j in range(8):
        named = jnp.where(probes_ref[j : j + 1, :] == lists, 1.0, named)
    before = lax.broadcasted_iota(jnp.int32, (32, 32), 0) <= lax.broadcasted_iota(jnp.int32, (32, 32), 1)
    count = named * jnp.dot(named.astype(BF16), before.astype(BF16), preferred_element_type=F32)
    place = place_matrix(slot_ref)
    table = lax.dot_general(count.astype(BF16), place, (((0,), (1,)), ((), ())), preferred_element_type=F32)
    table = (table - 1.0).astype(BF16)
    for copy in range(8):
        out_ref[copy, :, :D] = queries_ref[...]
        out_ref[copy, :, D:] = table


def find_wanted(probes_ref, slot_ref, pick_ref, group_ref):
    place = place_matrix(slot_ref)
    rank = rank_table(probes_ref, place)
    index = lax.broadcasted_iota(jnp.int32, (128, 32), 0)
    core = lax.axis_index("owner") & 1
    for j in range(8):
        placed = jnp.dot(place, (probes_ref[j : j + 1, :] == index).astype(BF16), preferred_element_type=F32)
        where = jnp.sum(placed * index.astype(F32), 0, keepdims=True).astype(jnp.int32)
        slot = jnp.sum(placed * rank, 0, keepdims=True).astype(jnp.int32)
        chip = where >> 3
        y_first, y_second = pairing_bits(chip >> 2, core, "y")
        x_first, x_second = pairing_bits(chip & 3, core, "x")
        row = (x_second * 8 + y_second * 4 + x_first * 2 + y_first) * 8 + (where & 4) + slot
        pick_ref[:, 32 * j : 32 * j + 32] = (index == row).astype(BF16)
        group_ref[:, 32 * j : 32 * j + 32] = jnp.broadcast_to(where & 3, (8, 32))


def lists_kernel(own, sibling, own_valid, sibling_valid, lists, norms, sems):
    copies = []
    for t in range(8):
        copies.append(pltpu.make_async_copy(own.at[t] if t < 4 else sibling.at[t - 4], lists.at[t], sems.at[t]))
        copies[t].start()
    row = lax.axis_index("replica") * 256 + lax.broadcasted_iota(jnp.int32, (256, 1), 0)
    lane = lax.broadcasted_iota(jnp.int32, (256, 128), 1)
    total = jnp.zeros((256, 128), F32)
    for t in (4, 5, 6, 7, 0, 1, 2, 3):
        copies[t].wait()
        rows = lists[t].astype(F32)
        valid = (own_valid if t < 4 else sibling_valid)[0:1, t % 4 : t % 4 + 1]
        norm = jnp.where(row < valid, 0.5 * jnp.sum(rows * rows, 1, keepdims=True), BIG)
        total = jnp.where(lane == t, norm, total)
    norms[...] = total


def chosen_queries(wide):
    chip = lax.axis_index("owner") // 2
    column = lax.broadcasted_iota(jnp.int32, (256, 128), 0)
    wanted = (lax.broadcasted_iota(jnp.int32, (256, 128), 1) == chip * 8 + (column >> 5)).astype(BF16)
    rank = lax.dot_general(wanted, wide[:, D:], (((1,), (1,)), ((), ())), preferred_element_type=F32)
    column = lax.broadcasted_iota(jnp.int32, (256, 256), 0)
    same_block = (lax.broadcasted_iota(jnp.int32, (256, 256), 1) >> 5) == ((column >> 2) & 7)
    pick = (same_block & (rank == (column & 3).astype(F32))).astype(BF16)
    return jnp.dot(pick, wide[:, :D], preferred_element_type=F32).astype(BF16)


def score(lists, norms, t, queries):
    return lax.dot_general(lists[t], queries, (((1,), (1,)), ((), ())), preferred_element_type=F32) - norms[:, t : t + 1]


def sort_rows(scores):
    return exchange([scores[8 * i : 8 * i + 8] for i in range(TOPK)], SORT_PAIRS)


def score_groups(groups, lists, norms, out, chosen, best):
    if len(groups) < 4:
        chosen[:, 32 * len(groups) :, :] = jnp.zeros((8, 128 - 32 * len(groups), D), BF16)
    for g, ref in enumerate(groups):
        picked = chosen_queries(ref[...])
        for t in range(8):
            chosen[t, 32 * g : 32 * g + 32, :] = picked[32 * t : 32 * t + 32]
    quads = []
    for quad in range(2):
        sets = [sort_rows(score(lists, norms, t, chosen[t])) for t in range(4 * quad, 4 * quad + 4)]
        quads.append(merged_rows(merged_rows(sets[0], sets[1], 1), merged_rows(sets[2], sets[3], 1), 2))
    for i, value in enumerate(merged_rows(quads[0], quads[1], 4)):
        best[8 * i : 8 * i + 8, :] = value
    for half in range(2):
        out[half] = jnp.concatenate([best[pl.ds(4 * half + t, TOPK, stride=8), :] for t in range(4)], 0).T


def first_kernel(*refs):
    score_groups(refs[:4], *refs[4:])


def second_kernel(*refs):
    groups, (lists, norms, probes, slots, out, pick, group, chosen, best) = refs[:3], refs[3:]
    score_groups(groups, lists, norms, out, chosen, best)
    find_wanted(probes, slots, pick, group)


def last_kernel(lower, upper, lists, norms, first, second, out, best):
    picked = chosen_queries(jnp.concatenate([lower[...], upper[...]], 0))
    lane = lax.broadcasted_iota(jnp.int32, (256, 128), 1)
    sets = []
    for half in range(2):
        queries = picked[128 * half : 128 * half + 128]
        scores = score(lists, norms, 4 * half, queries)
        for t in range(1, 4):
            scores = jnp.where((lane >> 5) == t, score(lists, norms, 4 * half + t, queries), scores)
        sets.append(sort_rows(scores))
    values = merged_rows(sets[0], sets[1], 1)
    for shift in (2, 4):
        values = merged(values, [pltpu.roll(value, 8 - shift, 0) for value in values])
    for i, value in enumerate(values):
        best[8 * i : 8 * i + 8, :] = value
    own = own_group()
    for half in range(2):
        rows = best[pl.ds(half, TOPK, stride=8), :]
        turned = jnp.concatenate([rows] + [pltpu.roll(rows, 128 - 32 * t, 1) for t in range(1, 4)], 0).T
        found = [(mask, first[half, 32 * g : 32 * g + 32, :]) for g, mask in enumerate(FIRST_HALF)]
        found += [(mask, second[half, 32 * g : 32 * g + 32, :]) for g, mask in enumerate(SECOND_HALF)]
        for mask, values in found + [(7, turned[:32])]:
            place = (own ^ mask) * 8
            for b in range(8):
                out[place + b, 4 * half : 4 * half + 4, :] = values[4 * b : 4 * b + 4]


def final_kernel(back_ref, pick_ref, group_ref, out_ref, tiles):
    pick = pick_ref[...]
    group = jnp.concatenate([group_ref[...]] * 4, 0)
    for z in range(4):
        left = back_ref[:, z >> 1, :, z & 1].reshape(128, 128).T
        found = jnp.zeros((128, 256), F32)
        for _ in range(3):
            piece = left.astype(BF16)
            left = left - piece.astype(F32)
            found = found + jnp.dot(piece, pick, preferred_element_type=F32)
        scores = found[:32]
        for t in range(1, 4):
            scores = jnp.where(group == t, found[32 * t : 32 * t + 32], scores)
        for half in range(2):
            tiles[pl.ds(2 * z + half, TOPK, stride=8), :] = scores[:, 128 * half : 128 * half + 128]
    values = [tiles[8 * i : 8 * i + 8, :] for i in range(TOPK)]
    for axis, shift in ((0, 4), (0, 2), (0, 1), (1, 64), (1, 32)):
        values = merged(values, [pltpu.roll(value, shift, axis) for value in values])
    row = lax.broadcasted_iota(jnp.int32, (8, 128), 0)
    ranked = []
    for first in range(0, TOPK, 8):
        rows = values[first]
        for i in range(1, 8):
            rows = jnp.where(row == i, values[first + i], rows)
        ranked.append(rows)
    out_ref[...] = jnp.concatenate(ranked, 0).T[:32]


def params():
    return pltpu.CompilerParams(vmem_limit_bytes=20 * 1024 * 1024)


def spaces(text):
    kinds = {"v": pltpu.VMEM, "s": pltpu.SMEM, "h": pltpu.HBM, "a": pl.ANY}
    return [pl.BlockSpec(memory_space=kinds[kind]) for kind in text]


def hop(value, mask):
    return lax.ppermute(value, AXES, [(device, far(device, mask, False)) for device in range(N_DEV)])


def per_device(queries, probes, list_slot, valid_rows, database):
    shape = jax.ShapeDtypeStruct
    slots = list_slot.reshape(1, 128)
    probes = probes.T
    wide = pl.pallas_call(
        widen_kernel, out_shape=pltpu.VMEM((8, 32, WIDE), BF16), in_specs=spaces("vvv"), out_specs=spaces("v")[0], name="widen"
    )(queries, probes, slots)
    near = lax.all_to_all(wide, AXES, 0, 0, axis_index_groups=NEAR_GROUPS, tiled=True).reshape(256, WIDE)
    sibling = lax.ppermute(database, AXES, CORE_SWAP)
    near, valid_rows = lax.optimization_barrier((near, valid_rows))
    sibling_valid = lax.ppermute(valid_rows, AXES, CORE_SWAP)

    groups = {0: near}
    for mask in (1, 2, 4):
        groups[mask] = hop(near, mask)
    lists, norms = pl.pallas_call(
        lists_kernel, out_shape=(pltpu.VMEM((8, 256, D), BF16), pltpu.VMEM((256, 128), F32)), in_specs=spaces("havv"),
        out_specs=spaces("vv"), scratch_shapes=[pltpu.SemaphoreType.DMA((8,))], compiler_params=params(), name="lists",
    )(pltpu.with_memory_space_constraint(database, pltpu.HBM), sibling, valid_rows.reshape(1, 4), sibling_valid.reshape(1, 4))
    groups[4], lists, norms = lax.optimization_barrier((groups[4], lists, norms))
    for mask, source, step in ((3, 1, 2), (6, 2, 4), (5, 4, 1)):
        groups[mask] = hop(groups[source], step)

    def scored(kernel, masks, more, out_shape, name):
        return pl.pallas_call(
            kernel, out_shape=out_shape, in_specs=spaces("v" * (len(masks) + 2 + len(more))), out_specs=spaces("v" * len(out_shape)),
            scratch_shapes=[pltpu.VMEM((8, 128, D), BF16), pltpu.VMEM((264, 128), F32)], compiler_params=params(), name=name,
        )(*[groups[mask] for mask in masks], lists, norms, *more)

    best_shape = pltpu.VMEM((2, 128, 128), F32)
    first, = scored(first_kernel, FIRST_HALF, (), (best_shape,), "score_first")
    groups[5], first = lax.optimization_barrier((groups[5], first))
    last = [hop(groups[5][:SPLIT], 2), hop(groups[3][SPLIT:], 4)]
    wanted_shapes = (pltpu.VMEM((128, 256), BF16), pltpu.VMEM((8, 256), jnp.int32))
    second, pick, group = scored(second_kernel, SECOND_HALF, (probes, slots), (best_shape, *wanted_shapes), "score_second")
    *last, second = lax.optimization_barrier((*last, second))
    blocks = pl.pallas_call(
        last_kernel, out_shape=shape((N_CORE, 8, 128), F32), in_specs=spaces("vvvvvv"), out_specs=spaces("v")[0],
        scratch_shapes=[pltpu.VMEM((264, 128), F32)], compiler_params=params(), name="score_last",
    )(*last, lists, norms, first, second)
    back = lax.all_to_all(blocks, AXES, 0, 0, axis_index_groups=CORE_GROUPS, tiled=True)
    return pl.pallas_call(
        final_kernel, out_shape=shape((32, TOPK), F32), in_specs=spaces("vvv"), out_specs=spaces("v")[0],
        scratch_shapes=[pltpu.VMEM((264, 128), F32)], compiler_params=params(), name="final",
    )(back.reshape(4, 2, 4, 2, 8, 128), pick, group)


def solution(mesh):
    in_specs = (P(AXES, None), P(AXES, None), P(), P("owner"), P("owner", "replica", None))
    return jax.shard_map(per_device, mesh=mesh, in_specs=in_specs, out_specs=P(AXES, None), check_vma=False)
```

```python
import jax
import jax.numpy as jnp
from jax import lax
from jax.experimental import pallas as pl
from jax.experimental.pallas import tpu as pltpu
from jax.sharding import PartitionSpec as P

D = 1024
WIDE = D + 128
TOPK = 32
AXES = ("owner", "replica")
N_DEV = 128
N_CORE = 64
BIG = 1e30
F32 = jnp.float32
BF16 = jnp.bfloat16

PAIRING = {"a": (1, 0, 3, 2), "b": (3, 2, 1, 0)}
DIMS_A = ("za", "ya", "xb")
DIMS_B = ("zb", "yb", "xa")


def moved(device, dim):
    z, core, x, y = device % 4, device // 4 % 2, device // 8 % 4, device // 32
    place = {"x": x, "y": y, "z": z}
    place[dim[0]] = PAIRING[dim[1]][place[dim[0]]]
    return ((place["y"] * 4 + place["x"]) * 2 + core) * 4 + place["z"]


def core_of(device):
    return device // 4 % 2


def dims_of(core, first):
    return DIMS_A if (core == 0) == first else DIMS_B


def far(device, mask, first):
    for bit, dim in enumerate(dims_of(core_of(device), first)):
        if mask >> bit & 1:
            device = moved(device, dim)
    return device


def at_address(core, address):
    return far(far(4 * core, address >> 3, False), address & 7, True)


CORE_GROUPS = [[at_address(core, address) for address in range(N_CORE)] for core in range(2)]
NEAR_GROUPS = [group[start : start + 8] for group in CORE_GROUPS for start in range(0, N_CORE, 8)]
CORE_SWAP = [(device, device ^ 4) for device in range(N_DEV)]
FIRST_HALF = (0, 1, 2, 4)
SECOND_HALF = (5, 3, 6)
SPLIT = 160


def pairing_bits(place, core, axis):
    low, high = (place ^ (place >> 1)) & 1, place >> 1
    low_first = jnp.equal(core, 0 if axis + "a" in DIMS_A else 1)
    return jnp.where(low_first, low, high), jnp.where(low_first, high, low)


def own_group():
    owner = lax.axis_index("owner")
    places = {"z": lax.axis_index("replica"), "y": owner >> 3, "x": (owner >> 1) & 3}
    z, y, x = [pairing_bits(place, owner & 1, axis)[1] for axis, place in places.items()]
    return z + 2 * y + 4 * x


def sort_pairs(count):
    pairs = []
    p = 1
    while p < count:
        k = p
        while k >= 1:
            for j in range(k % p, count - k, 2 * k):
                for i in range(min(k, count - j - k)):
                    if (i + j) // (p * 2) == (i + j + k) // (p * 2):
                        pairs.append((i + j, i + j + k))
            k //= 2
        p *= 2
    return pairs


SORT_PAIRS = sort_pairs(TOPK)
MERGE_PAIRS = [(i, i + d) for d in (16, 8, 4, 2, 1) for i in range(TOPK) if not i & d]


def exchange(values, pairs):
    values = list(values)
    for i, j in pairs:
        values[i], values[j] = jnp.maximum(values[i], values[j]), jnp.minimum(values[i], values[j])
    return values


def merged(first, second):
    return exchange([jnp.maximum(first[i], second[TOPK - 1 - i]) for i in range(TOPK)], MERGE_PAIRS)


def merged_rows(first, second, shift):
    row = lax.broadcasted_iota(jnp.int32, (8, 128), 0)
    odd = (row & shift) != 0
    here = [jnp.where(odd, b, a) for a, b in zip(first, second)]
    there = [pltpu.roll(jnp.where(odd, a, b), 8 - shift, 0) for a, b in zip(first, second)]
    return merged(here, there)


def place_matrix(slot_ref):
    core = lax.rem(lax.axis_index("owner"), 2)
    places = jnp.bitwise_xor(slot_ref[...], 4 * core)
    return (places == lax.broadcasted_iota(jnp.int32, (128, 128), 0)).astype(BF16)


def rank_table(probes_ref, place):
    lists = lax.broadcasted_iota(jnp.int32, (128, 32), 0)
    named = jnp.zeros((128, 32), F32)
    for j in range(8):
        named = jnp.where(probes_ref[j : j + 1, :] == lists, 1.0, named)
    probed = jnp.dot(place, named.astype(BF16), preferred_element_type=F32)
    before = lax.broadcasted_iota(jnp.int32, (32, 32), 0) < lax.broadcasted_iota(jnp.int32, (32, 32), 1)
    rank = jnp.dot(probed.astype(BF16), before.astype(BF16), preferred_element_type=F32)
    return jnp.where(probed > 0.5, rank, -1.0)


def widen_kernel(queries_ref, probes_ref, slot_ref, out_ref):
    lists = lax.broadcasted_iota(jnp.int32, (128, 32), 0)
    named = jnp.zeros((128, 32), F32)
    for j in range(8):
        named = jnp.where(probes_ref[j : j + 1, :] == lists, 1.0, named)
    before = lax.broadcasted_iota(jnp.int32, (32, 32), 0) <= lax.broadcasted_iota(jnp.int32, (32, 32), 1)
    count = named * jnp.dot(named.astype(BF16), before.astype(BF16), preferred_element_type=F32)
    place = place_matrix(slot_ref)
    table = lax.dot_general(count.astype(BF16), place, (((0,), (1,)), ((), ())), preferred_element_type=F32)
    table = (table - 1.0).astype(BF16)
    for copy in range(8):
        out_ref[copy, :, :D] = queries_ref[...]
        out_ref[copy, :, D:] = table


def find_wanted(probes_ref, slot_ref, pick_ref, group_ref):
    place = place_matrix(slot_ref)
    rank = rank_table(probes_ref, place)
    index = lax.broadcasted_iota(jnp.int32, (128, 32), 0)
    core = lax.axis_index("owner") & 1
    for j in range(8):
        placed = jnp.dot(place, (probes_ref[j : j + 1, :] == index).astype(BF16), preferred_element_type=F32)
        where = jnp.sum(placed * index.astype(F32), 0, keepdims=True).astype(jnp.int32)
        slot = jnp.sum(placed * rank, 0, keepdims=True).astype(jnp.int32)
        chip = where >> 3
        y_first, y_second = pairing_bits(chip >> 2, core, "y")
        x_first, x_second = pairing_bits(chip & 3, core, "x")
        row = (x_second * 8 + y_second * 4 + x_first * 2 + y_first) * 8 + (where & 4) + slot
        pick_ref[:, 32 * j : 32 * j + 32] = (index == row).astype(BF16)
        group_ref[:, 32 * j : 32 * j + 32] = jnp.broadcast_to(where & 3, (8, 32))


def lists_kernel(own, sibling, own_rows, sibling_valid, lists, norms, own_valid, sems):
    copies = []
    for t in range(8):
        copies.append(pltpu.make_async_copy(own.at[t] if t < 4 else sibling.at[t - 4], lists.at[t], sems.at[t]))
        copies[t].start()
    valid_copy = pltpu.make_async_copy(own_rows, own_valid, sems.at[8])
    valid_copy.start()
    row = lax.axis_index("replica") * 256 + lax.broadcasted_iota(jnp.int32, (256, 1), 0)
    lane = lax.broadcasted_iota(jnp.int32, (256, 128), 1)
    total = jnp.zeros((256, 128), F32)
    for t in (4, 5, 6, 7, 0, 1, 2, 3):
        if t == 0:
            valid_copy.wait()
        copies[t].wait()
        rows = lists[t].astype(F32)
        valid = (own_valid if t < 4 else sibling_valid)[0:1, t % 4 : t % 4 + 1]
        norm = jnp.where(row < valid, 0.5 * jnp.sum(rows * rows, 1, keepdims=True), BIG)
        total = jnp.where(lane == t, norm, total)
    norms[...] = total


def chosen_queries(wide):
    chip = lax.axis_index("owner") // 2
    column = lax.broadcasted_iota(jnp.int32, (256, 128), 0)
    wanted = (lax.broadcasted_iota(jnp.int32, (256, 128), 1) == chip * 8 + (column >> 5)).astype(BF16)
    rank = lax.dot_general(wanted, wide[:, D:], (((1,), (1,)), ((), ())), preferred_element_type=F32)
    column = lax.broadcasted_iota(jnp.int32, (256, 256), 0)
    same_block = (lax.broadcasted_iota(jnp.int32, (256, 256), 1) >> 5) == ((column >> 2) & 7)
    pick = (same_block & (rank == (column & 3).astype(F32))).astype(BF16)
    return jnp.dot(pick, wide[:, :D], preferred_element_type=F32).astype(BF16)


def score(lists, norms, t, queries):
    return lax.dot_general(lists[t], queries, (((1,), (1,)), ((), ())), preferred_element_type=F32) - norms[:, t : t + 1]


def sort_rows(scores):
    return exchange([scores[8 * i : 8 * i + 8] for i in range(TOPK)], SORT_PAIRS)


def score_groups(groups, lists, norms, out, chosen, best):
    if len(groups) < 4:
        chosen[:, 32 * len(groups) :, :] = jnp.zeros((8, 128 - 32 * len(groups), D), BF16)
    for g, ref in enumerate(groups):
        picked = chosen_queries(ref[...])
        for t in range(8):
            chosen[t, 32 * g : 32 * g + 32, :] = picked[32 * t : 32 * t + 32]
    quads = []
    for quad in range(2):
        sets = [sort_rows(score(lists, norms, t, chosen[t])) for t in range(4 * quad, 4 * quad + 4)]
        quads.append(merged_rows(merged_rows(sets[0], sets[1], 1), merged_rows(sets[2], sets[3], 1), 2))
    for i, value in enumerate(merged_rows(quads[0], quads[1], 4)):
        best[8 * i : 8 * i + 8, :] = value
    for half in range(2):
        out[half] = jnp.concatenate([best[pl.ds(4 * half + t, TOPK, stride=8), :] for t in range(4)], 0).T


def first_kernel(*refs):
    score_groups(refs[:4], *refs[4:])


def second_kernel(*refs):
    groups, (lists, norms, probes, slots, out, pick, group, chosen, best) = refs[:3], refs[3:]
    score_groups(groups, lists, norms, out, chosen, best)
    find_wanted(probes, slots, pick, group)


def last_kernel(lower, upper, lists, norms, first, second, out, best):
    picked = chosen_queries(jnp.concatenate([lower[...], upper[...]], 0))
    lane = lax.broadcasted_iota(jnp.int32, (256, 128), 1)
    sets = []
    for half in range(2):
        queries = picked[128 * half : 128 * half + 128]
        scores = score(lists, norms, 4 * half, queries)
        for t in range(1, 4):
            scores = jnp.where((lane >> 5) == t, score(lists, norms, 4 * half + t, queries), scores)
        sets.append(sort_rows(scores))
    values = merged_rows(sets[0], sets[1], 1)
    for shift in (2, 4):
        values = merged(values, [pltpu.roll(value, 8 - shift, 0) for value in values])
    for i, value in enumerate(values):
        best[8 * i : 8 * i + 8, :] = value
    own = own_group()
    for half in range(2):
        rows = best[pl.ds(half, TOPK, stride=8), :]
        turned = jnp.concatenate([rows] + [pltpu.roll(rows, 128 - 32 * t, 1) for t in range(1, 4)], 0).T
        found = [(mask, first[half, 32 * g : 32 * g + 32, :]) for g, mask in enumerate(FIRST_HALF)]
        found += [(mask, second[half, 32 * g : 32 * g + 32, :]) for g, mask in enumerate(SECOND_HALF)]
        for mask, values in found + [(7, turned[:32])]:
            place = (own ^ mask) * 8
            for b in range(8):
                out[place + b, 4 * half : 4 * half + 4, :] = values[4 * b : 4 * b + 4]


def final_kernel(back_ref, pick_ref, group_ref, out_ref, tiles):
    pick = pick_ref[...]
    group = jnp.concatenate([group_ref[...]] * 4, 0)
    for z in range(4):
        left = back_ref[:, z >> 1, :, z & 1].reshape(128, 128).T
        found = jnp.zeros((128, 256), F32)
        for _ in range(3):
            piece = left.astype(BF16)
            left = left - piece.astype(F32)
            found = found + jnp.dot(piece, pick, preferred_element_type=F32)
        scores = found[:32]
        for t in range(1, 4):
            scores = jnp.where(group == t, found[32 * t : 32 * t + 32], scores)
        for half in range(2):
            tiles[pl.ds(2 * z + half, TOPK, stride=8), :] = scores[:, 128 * half : 128 * half + 128]
    values = [tiles[8 * i : 8 * i + 8, :] for i in range(TOPK)]
    for axis, shift in ((0, 4), (0, 2), (0, 1), (1, 64), (1, 32)):
        values = merged(values, [pltpu.roll(value, shift, axis) for value in values])
    row = lax.broadcasted_iota(jnp.int32, (8, 128), 0)
    ranked = []
    for first in range(0, TOPK, 8):
        rows = values[first]
        for i in range(1, 8):
            rows = jnp.where(row == i, values[first + i], rows)
        ranked.append(rows)
    out_ref[...] = jnp.concatenate(ranked, 0).T[:32]


def params():
    return pltpu.CompilerParams(vmem_limit_bytes=20 * 1024 * 1024)


def spaces(text):
    kinds = {"v": pltpu.VMEM, "s": pltpu.SMEM, "h": pltpu.HBM, "a": pl.ANY}
    return [pl.BlockSpec(memory_space=kinds[kind]) for kind in text]


def hop(value, mask):
    return lax.ppermute(value, AXES, [(device, far(device, mask, False)) for device in range(N_DEV)])


def per_device(queries, probes, list_slot, valid_rows, database):
    shape = jax.ShapeDtypeStruct
    slots = list_slot.reshape(1, 128)
    probes = probes.T
    wide = pl.pallas_call(
        widen_kernel, out_shape=pltpu.VMEM((8, 32, WIDE), BF16), in_specs=spaces("vvv"), out_specs=spaces("v")[0], name="widen"
    )(queries, probes, slots)
    near = lax.all_to_all(wide, AXES, 0, 0, axis_index_groups=NEAR_GROUPS, tiled=True).reshape(256, WIDE)
    sibling = lax.ppermute(database, AXES, CORE_SWAP)
    near, valid_rows = lax.optimization_barrier((near, valid_rows))
    sibling_valid = lax.ppermute(valid_rows, AXES, CORE_SWAP)

    groups = {0: near}
    for mask in (1, 2, 4):
        groups[mask] = hop(near, mask)
    lists, norms = pl.pallas_call(
        lists_kernel, out_shape=(pltpu.VMEM((8, 256, D), BF16), pltpu.VMEM((256, 128), F32)), in_specs=spaces("hahv"),
        out_specs=spaces("vv"), scratch_shapes=[pltpu.VMEM((1, 4), jnp.int32), pltpu.SemaphoreType.DMA((9,))], compiler_params=params(), name="lists",
    )(pltpu.with_memory_space_constraint(database, pltpu.HBM), sibling, pltpu.with_memory_space_constraint(valid_rows.reshape(1, 4), pltpu.HBM), sibling_valid.reshape(1, 4))
    groups[4], lists, norms = lax.optimization_barrier((groups[4], lists, norms))
    for mask, source, step in ((3, 1, 2), (6, 2, 4), (5, 4, 1)):
        groups[mask] = hop(groups[source], step)

    def scored(kernel, masks, more, out_shape, name):
        return pl.pallas_call(
            kernel, out_shape=out_shape, in_specs=spaces("v" * (len(masks) + 2 + len(more))), out_specs=spaces("v" * len(out_shape)),
            scratch_shapes=[pltpu.VMEM((8, 128, D), BF16), pltpu.VMEM((264, 128), F32)], compiler_params=params(), name=name,
        )(*[groups[mask] for mask in masks], lists, norms, *more)

    best_shape = pltpu.VMEM((2, 128, 128), F32)
    first, = scored(first_kernel, FIRST_HALF, (), (best_shape,), "score_first")
    groups[5], first = lax.optimization_barrier((groups[5], first))
    last = [hop(groups[5][:SPLIT], 2), hop(groups[3][SPLIT:], 4)]
    wanted_shapes = (pltpu.VMEM((128, 256), BF16), pltpu.VMEM((8, 256), jnp.int32))
    second, pick, group = scored(second_kernel, SECOND_HALF, (probes, slots), (best_shape, *wanted_shapes), "score_second")
    *last, second = lax.optimization_barrier((*last, second))
    blocks = pl.pallas_call(
        last_kernel, out_shape=shape((N_CORE, 8, 128), F32), in_specs=spaces("vvvvvv"), out_specs=spaces("v")[0],
        scratch_shapes=[pltpu.VMEM((264, 128), F32)], compiler_params=params(), name="score_last",
    )(*last, lists, norms, first, second)
    back = lax.all_to_all(blocks, AXES, 0, 0, axis_index_groups=CORE_GROUPS, tiled=True)
    return pl.pallas_call(
        final_kernel, out_shape=shape((32, TOPK), F32), in_specs=spaces("vvv"), out_specs=spaces("v")[0],
        scratch_shapes=[pltpu.VMEM((264, 128), F32)], compiler_params=params(), name="final",
    )(back.reshape(4, 2, 4, 2, 8, 128), pick, group)


def solution(mesh):
    in_specs = (P(AXES, None), P(AXES, None), P(), P("owner"), P("owner", "replica", None))
    return jax.shard_map(per_device, mesh=mesh, in_specs=in_specs, out_specs=P(AXES, None), check_vma=False)
```
